256 devices in a mesh: ctx: 32 (over y, z_hi, x), exp: 8 (over z_lo, core).
Axes of the slice: x: 4, y: 4, z: 8 (z_hi: 2, z_lo: 4; z = z_hi * 4 + z_lo), core: 2. Of those that a mesh axis runs over, the one named last changes fastest.
Arguments:
- resid: bfloat16 [4096, 4096], P('ctx'), may hold values from -6 to 6
- out_grad: bfloat16 [4096, 4096], P('ctx'), may hold values from -6 to 6
- norm_gain: float32 [4096], replicated, may hold values from 0.1 to 1.9
- expert_ids: int32 [4096, 8], P('ctx'), may hold values from 0 to 127, all different within a row; in each aligned block of 128 rows (0 to 127, 128 to 255, ...) at most 16 rows name the same one
- combine: float32 [4096, 8], P('ctx'), may hold values from 0.3 to 1.2
- w_gate: bfloat16 [4096, 1536], P(None, 'exp'), may hold values from -0.09375 to 0.09375
- w_up: bfloat16 [4096, 1536], P(None, 'exp'), may hold values from -0.09375 to 0.09375
- w_down: bfloat16 [1536, 4096], P('exp'), may hold values from -0.15625 to 0.15625
- w_out: bfloat16 [4096, 4096], P('exp'), may hold values from -0.09375 to 0.09375
- queries: bfloat16 [4096, 4096], P('ctx', 'exp'), may hold values from -6 to 6
- keys: bfloat16 [4096, 256], P('ctx'), may hold values from -6 to 6
- values: bfloat16 [4096, 256], P('ctx'), may hold values from -6 to 6
- span_order: int32 [64], replicated, may hold values from 0 to 63, each once
Outputs:
- resid_grad: bfloat16 [4096, 4096], P('ctx')
- query_grad: bfloat16 [4096, 4096], P('ctx', 'exp')
- key_grad: bfloat16 [4096, 256], P(('ctx', 'exp'))
- value_grad: bfloat16 [4096, 256], P(('ctx', 'exp'))
The draws below stay inside these ranges and needn't reach their ends.
Inputs may be any that keep to these rules, and one draw needn't show every extreme that they name: `expert_ids`: the 8 entries of a token differ; among the 128 stored rows of one index of ctx at most 16 name any one expert. `span_order`: each block of positions appears once.
All inputs are finite; a program needn't handle non-finite values.
Results may differ from the reference program's by a relative error of at most 0.013.
Values may be sent and summed in bfloat16 or wider, within the bound.
No kernel may reach another device: no remote copies, remote signals or barrier semaphores. Data moves between devices by JAX's collectives and lax.ppermute only.
A program may use at most 128 MiB of HBM per device.

```python
import math
import jax
import jax.numpy as jnp
import numpy as np
from jax import lax

D = 4096
FF = 1536
EXPERTS = 128
TOP = 8
DH = 128
GROUP = 16
S_DEV = 128
SEQ = 4096
CH = 64
CAP = 16
HQ = 32
KVH = 2
N_CTX = 32


def draw_queries(key, part):
    key = jax.random.fold_in(key, 3)
    drawn = jax.random.truncated_normal(key, -6.0, 6.0, (SEQ, HQ, DH), jnp.float32)
    return drawn.reshape(SEQ, HQ * DH).astype(jnp.bfloat16)


def draw_keys(key, part):
    key = jax.random.fold_in(key, 5)
    drawn = jax.random.truncated_normal(key, -6.0, 6.0, (SEQ, KVH, DH), jnp.float32)
    return drawn.reshape(SEQ, KVH * DH).astype(jnp.bfloat16)


def block_levels(key, extent, shards, least, top_value):
    gain, own = 1.0, jax.random.fold_in(key, 6)
    for dim, blocks in shards:
        heights = jnp.exp(jax.random.uniform(jax.random.fold_in(own, dim), (blocks,), jnp.float32, least / len(shards), top_value / len(shards)))
        gain = gain * jnp.repeat(heights, extent[dim] // blocks).reshape([-1 if axis == dim else 1 for axis in range(len(extent))])
    return gain


def assign_block(own_key, own, number, rows, count, top, bound, slope):
    ranking = jax.random.permutation(own_key, count)
    heavy_load, usual = portions_of(count, rows * top, bound, slope, True), portions_of(count, rows * top, bound, slope, False)
    places = jnp.arange(count)

    def named(lengths, rotation):
        used = int((lengths > 0).sum())
        fixed = max(1, used // 4)
        passed = fixed + (places - fixed + rotation * (used - fixed)) % max(1, count - fixed)
        return jnp.zeros((count,), jnp.int32).at[ranking[jnp.where(places < fixed, places, passed)]].set(jnp.asarray(lengths, jnp.int32))

    lengths = jnp.where(number % 4 == 0, named(heavy_load, number // 4), named(usual, number - number // 4 - 1))
    mixed = jax.random.permutation(jax.random.fold_in(own, 3), count)
    donor, sink = mixed[0:count // 2 * 2:2], mixed[1:count // 2 * 2:2]
    room = jnp.minimum(lengths[donor] - 1, bound - lengths[sink]) // 2
    room = jnp.where((donor == ranking[0]) | (sink == ranking[0]) | (lengths[sink] == 0), 0, jnp.maximum(room, 0))
    passed = jax.random.randint(jax.random.fold_in(own, 4), (count // 2,), 0, 1 << 20) % (room + 1)
    lengths = lengths.at[donor].add(-passed).at[sink].add(passed)
    members = jnp.searchsorted(jnp.cumsum(lengths), jnp.arange(rows * top), side="right").astype(jnp.int32)
    listing = members.reshape(top, rows).T
    listing = listing[jax.random.permutation(jax.random.fold_in(own, 1), rows)]
    rotation = jax.random.randint(jax.random.fold_in(own, 2), (rows, 1), 0, top)
    return jnp.take_along_axis(listing, (jnp.arange(top)[None, :] + rotation) % top, axis=1)


def portions_of(number_of, total, most, slope, full):
    portions = [(1 << 20) // math.isqrt(standing ** slope) + 1 for standing in range(1, number_of + 1)]
    largest = most if full else min(most, max(-(-total // number_of), total * portions[0] // sum(portions)))
    least = 1 if total - largest >= number_of - 1 else 0
    given, surplus = [largest] + [least] * (number_of - 1), total - largest - least * (number_of - 1)
    while surplus > 0:
        free = [i for i in range(1, number_of) if given[i] < largest] or [i for i in range(1, number_of) if given[i] < most]
        whole, budget = sum([portions[i] for i in free]), surplus
        for i in free:
            more = min(most - given[i], max(1, budget * portions[i] // whole), surplus)
            given[i] = given[i] + more
            surplus = surplus - more
    return np.array(given)


def bell_draw(key, extent, spread, reach, pieces=(), held_as=jnp.bfloat16):
    values = jax.random.normal(key, extent, jnp.float32) * spread
    if len(pieces) > 0:
        values = block_levels(key, extent, pieces, -0.22, 0.18) * values
    return jnp.clip(values, min=-reach, max=reach).astype(held_as)


def setup_inputs(seed: int = 0) -> dict:
    splits = jax.random.split(jax.random.key(seed), 14)
    resid = bell_draw(splits[0], (SEQ, D), 1.0, 6.0, ((0, 32),))
    out_grad = bell_draw(splits[1], (SEQ, D), 1.0, 6.0, ((0, 32),))
    norm_gain = jnp.clip(1.0 + 0.18 * jax.random.normal(splits[2], (D,), jnp.float32), 0.1, 1.9)
    expert_ids_keys = jax.random.split(jax.random.fold_in(splits[3], 1), SEQ // S_DEV)
    expert_ids_turns = jax.random.permutation(jax.random.fold_in(splits[3], 3), SEQ // S_DEV)
    expert_ids = jax.vmap(lambda own, number: assign_block(jax.random.fold_in(splits[3], 2), own, number, S_DEV, EXPERTS, TOP, CAP, 2))(expert_ids_keys, expert_ids_turns).reshape((SEQ, TOP))
    combine = jnp.clip(0.3 + 0.90000004 * jax.random.uniform(splits[4], (SEQ, TOP), jnp.float32) ** block_levels(splits[4], (SEQ, TOP), ((0, 32),), -0.2, 0.2), 0.3, 1.2)
    w_gate = bell_draw(splits[5], (D, FF), D ** -0.5, 0.09375, ((1, 8),))
    w_up = bell_draw(splits[6], (D, FF), D ** -0.5, 0.09375, ((1, 8),))
    w_down = bell_draw(splits[7], (FF, D), FF ** -0.5, 0.15625, ((0, 8),))
    w_out = bell_draw(splits[8], (HQ * DH, D), D ** -0.5, 0.09375, ((0, 8),))
    queries = draw_queries(jax.random.fold_in(splits[13], 71), 0)
    keys = draw_keys(jax.random.fold_in(splits[13], 71), 0)
    values = bell_draw(splits[11], (SEQ, KVH * DH), 1.0, 6.0, ((0, 32),))
    span_order = jax.random.permutation(splits[12], 2 * N_CTX).astype(jnp.int32)
    return {"resid": resid, "out_grad": out_grad, "norm_gain": norm_gain, "expert_ids": expert_ids, "combine": combine, "w_gate": w_gate, "w_up": w_up, "w_down": w_down, "w_out": w_out, "queries": queries, "keys": keys, "values": values, "span_order": span_order}


eps_norm = 1e-06

def contract_last(left, right):
    return lax.dot_general(left, right, (((1,), (1,)), ((), ())), preferred_element_type=jnp.float32)

def expert_grads(normed_rows, grad_rows, w_gate, w_up, w_down):
    gate_pre = jnp.dot(normed_rows, w_gate, preferred_element_type=jnp.float32)
    up_pre = jnp.dot(normed_rows, w_up, preferred_element_type=jnp.float32)
    hidden_grad = contract_last(grad_rows, w_down)
    sig_gate = jax.nn.sigmoid(gate_pre)
    gate_grad = (hidden_grad * up_pre * sig_gate * (1.0 + gate_pre * (1.0 - sig_gate))).astype(jnp.bfloat16)
    up_grad = (hidden_grad * gate_pre * sig_gate).astype(jnp.bfloat16)
    return contract_last(gate_grad, w_gate) + contract_last(up_grad, w_up)

def reference(resid, out_grad, norm_gain, expert_ids, combine, w_gate, w_up, w_down, w_out, queries, keys, values, span_order):
    resid_wide = resid.astype(jnp.float32)
    rms_scale = lax.rsqrt(lax.optimization_barrier(jnp.mean(resid_wide * resid_wide, axis=1, keepdims=True)) + eps_norm)
    normed = (resid_wide * rms_scale * norm_gain).astype(jnp.bfloat16)
    expert_weight = lax.optimization_barrier(jnp.sum(jnp.where(expert_ids == 0, combine, jnp.zeros_like(combine)), axis=1))
    scaled_grad = (out_grad.astype(jnp.float32) * expert_weight[:, None]).astype(jnp.bfloat16)
    chosen = jnp.any(expert_ids == 0, axis=1)
    picked = jnp.nonzero(chosen, size=N_CTX * CAP, fill_value=0)[0].astype(jnp.int32)
    valid = jnp.arange(N_CTX * CAP, dtype=jnp.int32) < jnp.sum(chosen.astype(jnp.int32))
    row_grads = expert_grads(normed[picked], scaled_grad[picked], w_gate, w_up, w_down)
    row_grads = jnp.where(valid[:, None], row_grads, jnp.zeros_like(row_grads))
    normed_grad = jnp.zeros((SEQ, D), jnp.float32).at[picked].add(row_grads)
    gained = normed_grad * norm_gain
    inner = lax.optimization_barrier(jnp.mean(gained * resid_wide, axis=1, keepdims=True))
    resid_grad = (out_grad.astype(jnp.float32) + rms_scale * (gained - resid_wide * rms_scale * rms_scale * inner)).astype(jnp.bfloat16)
    attn_grad = contract_last(resid_grad, w_out).astype(jnp.bfloat16)
    key_pos = (span_order[:, None] * CH + jnp.arange(CH, dtype=jnp.int32)[None, :]).reshape(-1)
    allowed = key_pos[None, :] <= key_pos[:, None]
    scale = 1.0 / math.sqrt(DH)

    def head_grads(operands):
        query_head, grad_head, key_head, value_head = operands
        scores = contract_last(query_head, key_head) * scale
        scores = jnp.where(allowed, scores, -jnp.inf)
        row_max = lax.optimization_barrier(jnp.max(scores, axis=1, keepdims=True))
        log_total = row_max + jnp.log(lax.optimization_barrier(jnp.sum(jnp.exp(scores - row_max), axis=1, keepdims=True)))
        probs = jnp.exp(scores - log_total)
        probs_low = probs.astype(jnp.bfloat16)
        attn_out = jnp.dot(probs_low, value_head, preferred_element_type=jnp.float32)
        delta = lax.optimization_barrier(jnp.sum(grad_head.astype(jnp.float32) * attn_out, axis=1, keepdims=True))
        prob_grad = contract_last(grad_head, value_head)
        score_grad = (probs * (prob_grad - delta)).astype(jnp.bfloat16)
        head_query = jnp.dot(score_grad, key_head, preferred_element_type=jnp.float32) * scale
        head_key = jnp.dot(score_grad.T, query_head, preferred_element_type=jnp.float32) * scale
        head_value = jnp.dot(probs_low.T, grad_head, preferred_element_type=jnp.float32)
        return (head_query, head_key, head_value)
    query_heads = queries.reshape(SEQ, HQ, DH).transpose(1, 0, 2)
    grad_heads = attn_grad.reshape(SEQ, HQ, DH).transpose(1, 0, 2)
    group_of = jnp.arange(HQ, dtype=jnp.int32) // GROUP
    key_heads = keys.reshape(SEQ, KVH, DH).transpose(1, 0, 2)[group_of]
    value_heads = values.reshape(SEQ, KVH, DH).transpose(1, 0, 2)[group_of]
    query_parts, key_parts, value_parts = lax.map(head_grads, (query_heads, grad_heads, key_heads, value_heads))
    query_grad = query_parts.transpose(1, 0, 2).reshape(SEQ, HQ * DH).astype(jnp.bfloat16)
    key_grad = jnp.concatenate([lax.optimization_barrier(jnp.sum(key_parts[group * GROUP:min((group + 1) * GROUP, HQ)], axis=0)) for group in range(KVH)], axis=1).astype(jnp.bfloat16)
    value_grad = jnp.concatenate([lax.optimization_barrier(jnp.sum(value_parts[group * GROUP:min((group + 1) * GROUP, HQ)], axis=0)) for group in range(KVH)], axis=1).astype(jnp.bfloat16)
    return (resid_grad, query_grad, key_grad, value_grad)
```

```python
import math

import jax
import jax.numpy as jnp
from jax import lax
from jax.sharding import PartitionSpec as P

DH = 128
GROUP = 16
CAP = 16
EPS = 1e-06
LOW = -1e30

bf16 = jnp.bfloat16
f32 = jnp.float32


def contract_last(left, right):
    return lax.dot_general(left, right, (((1,), (1,)), ((), ())), preferred_element_type=f32)


def contract_first(left, right):
    return lax.dot_general(left, right, (((0,), (0,)), ((), ())), preferred_element_type=f32)


def dot(left, right):
    return jnp.dot(left, right, preferred_element_type=f32)


def across(array, mask):
    count = lax.axis_size("exp")
    return lax.ppermute(array, "exp", [(i, i ^ mask) for i in range(count)])


def on_device(
    resid,
    out_grad,
    norm_gain,
    expert_ids,
    combine,
    w_gate,
    w_up,
    w_down,
    w_out,
    queries,
    keys,
    values,
    span_order,
):
    rows, width = resid.shape
    heads = queries.shape[1] // DH
    n_ctx = lax.axis_size("ctx")
    n_exp = lax.axis_size("exp")
    ctx, exp = lax.axis_index("ctx"), lax.axis_index("exp")
    core, z_lo = exp % 2, exp // 2
    chunk = rows // n_exp
    n_z = n_exp // 2
    block = rows // 2
    scale = 1.0 / math.sqrt(DH)

    kv_index = exp * heads // GROUP
    own_kv = jnp.concatenate(
        [
            lax.dynamic_slice_in_dim(keys, kv_index * DH, DH, 1),
            lax.dynamic_slice_in_dim(values, kv_index * DH, DH, 1),
        ],
        axis=1,
    ).reshape(n_z, 2, chunk, 2 * DH)
    mine = jnp.where(core == 0, own_kv[:, 0], own_kv[:, 1]).reshape(n_z * chunk, 2 * DH)
    sent = jnp.broadcast_to(mine[None], (n_ctx,) + mine.shape)
    kv = lax.all_to_all(sent, "ctx", 0, 0, tiled=True).reshape(-1, 2 * DH)
    k_all, v_all = kv[:, :DH], kv[:, DH:]
    q_own = queries
    q_par = across(queries, 1)

    chosen = jnp.any(expert_ids == 0, axis=1)
    weight = jnp.sum(jnp.where(expert_ids == 0, combine, 0.0), axis=1)
    rank = jnp.cumsum(chosen.astype(jnp.int32)) - 1
    slots = lax.iota(jnp.int32, CAP)
    picks = (rank[None, :] == slots[:, None]) & chosen[None, :]
    selector = picks.astype(bf16)
    weight16 = jnp.sum(jnp.where(picks, weight[None, :], 0.0), axis=1, keepdims=True)
    resid16 = dot(selector, resid)
    grad16 = dot(selector, out_grad)
    rms16 = lax.rsqrt(jnp.mean(resid16 * resid16, axis=1, keepdims=True) + EPS)
    normed16 = (resid16 * rms16 * norm_gain).astype(bf16)
    scaled16 = (grad16 * weight16).astype(bf16)
    gate_pre = dot(normed16, w_gate)
    up_pre = dot(normed16, w_up)
    hidden = contract_last(scaled16, w_down)
    sig = jax.nn.sigmoid(gate_pre)
    gate_grad = (hidden * up_pre * sig * (1.0 + gate_pre * (1.0 - sig))).astype(bf16)
    up_grad = (hidden * gate_pre * sig).astype(bf16)
    partial = contract_last(gate_grad, w_gate) + contract_last(up_grad, w_up)

    half = width // 2
    left, right = partial[:, :half], partial[:, half:]
    keep = jnp.where(core == 0, left, right)
    give = jnp.where(core == 0, right, left).astype(bf16)
    pair = lax.optimization_barrier((keep + across(give, 1).astype(f32)).astype(bf16))
    r1, r2, r3 = across(pair, 2), across(pair, 4), across(pair, 6)
    total = (pair.astype(f32) + r1.astype(f32)) + (r2.astype(f32) + r3.astype(f32))
    total = lax.optimization_barrier(total.astype(bf16))
    other = across(total, 1)
    normed_grad = jnp.concatenate(
        [jnp.where(core == 0, total, other), jnp.where(core == 0, other, total)], axis=1
    ).astype(f32)
    gained = normed_grad * norm_gain
    inner = jnp.mean(gained * resid16, axis=1, keepdims=True)
    rows16 = (grad16 + rms16 * (gained - resid16 * rms16 * rms16 * inner)).astype(bf16)

    base_own = contract_last(out_grad, w_out).astype(bf16)
    base_par = across(base_own, 1)
    late_own = contract_last(rows16, w_out).astype(bf16)
    late_par = across(late_own, 1)
    resid_grad = jnp.where(
        chosen[:, None], contract_first(selector, rows16).astype(bf16), out_grad
    )
    d_own = jnp.where(chosen[:, None], contract_first(selector, late_own).astype(bf16), base_own)
    d_par = jnp.where(chosen[:, None], contract_first(selector, late_par).astype(bf16), base_par)

    def by_head(own, par):
        both = jnp.concatenate([own, par], axis=1)
        return both.reshape(rows, 2 * heads, DH).swapaxes(0, 1).reshape(2 * heads * rows, DH)

    spans = span_order.reshape(n_ctx, 2)
    place = lax.iota(jnp.int32, rows)
    row_pos = spans[:, :, None] * block + lax.iota(jnp.int32, block)
    query_pos = lax.dynamic_index_in_dim(row_pos, ctx, 0, keepdims=False).reshape(rows)
    split_pos = row_pos.reshape(n_ctx, n_z, 2, chunk)
    key_pos = jnp.where(core == 0, split_pos[:, :, 0], split_pos[:, :, 1]).reshape(-1)
    allowed = key_pos[None, :] <= query_pos[:, None]
    n_keys = key_pos.shape[0]
    q = by_head(q_own, q_par)
    scores = contract_last(q, k_all) * scale
    scores = jnp.where(
        allowed[None], scores.reshape(2 * heads, rows, n_keys), LOW
    )
    top = jnp.max(scores, axis=2)
    weights = jnp.exp(scores - top[..., None])
    mass = jnp.sum(weights, axis=2)
    out_part = dot(weights.astype(bf16).reshape(-1, n_keys), v_all).reshape(2 * heads, rows, DH)
    stats = jnp.stack([top, mass])
    stats_par = across(jnp.concatenate([stats[:, heads:], stats[:, :heads]], axis=1), 1)
    out_low = out_part.astype(bf16)
    out_par = across(jnp.concatenate([out_low[heads:], out_low[:heads]], axis=0), 1)
    peak = jnp.maximum(top, stats_par[0])
    near, far = jnp.exp(top - peak), jnp.exp(stats_par[0] - peak)
    inverse = 1.0 / (mass * near + stats_par[1] * far)
    out = (out_part * (near * inverse)[..., None]) + out_par.astype(f32) * (far * inverse)[..., None]
    probs = weights * (near * inverse)[..., None]
    probs_low = probs.astype(bf16).reshape(-1, n_keys)

    d = by_head(d_own, d_par)
    delta = jnp.sum(d.astype(f32) * out.reshape(-1, DH), axis=1)
    prob_grad = contract_last(d, v_all)
    score_grad = (probs.reshape(-1, n_keys) * (prob_grad - delta[:, None])).astype(bf16)
    key_part = contract_first(score_grad, q) * scale
    value_part = contract_first(probs_low, d)
    kv_part = jnp.concatenate([key_part, value_part], axis=1).astype(bf16)
    got = lax.all_to_all(
        kv_part.reshape(n_ctx, n_z * chunk, 2 * DH), "ctx", 0, 0, tiled=True
    )
    query_part = (dot(score_grad, k_all) * scale).reshape(2 * heads, rows, DH).swapaxes(0, 1)
    query_part = query_part.reshape(rows, 2 * heads * DH)
    query_give = query_part[:, heads * DH :].astype(bf16)
    query_grad = (query_part[:, : heads * DH] + across(query_give, 1).astype(f32)).astype(bf16)

    owned = jnp.sum(got.astype(f32), axis=0).reshape(n_z, chunk, 2 * DH)

    def chunk_of(index):
        return lax.dynamic_index_in_dim(owned, index, 0, keepdims=False)

    same = chunk_of(z_lo) + across(chunk_of(z_lo ^ 1), 2)
    rest = across(chunk_of(z_lo ^ 2), 4) + across(chunk_of(z_lo ^ 3), 6)
    first = jnp.where(z_lo < n_z // 2, same, rest)
    second = jnp.where(z_lo < n_z // 2, rest, same)
    key_grad = jnp.concatenate([first[:, :DH], second[:, :DH]], axis=1).astype(bf16)
    value_grad = jnp.concatenate([first[:, DH:], second[:, DH:]], axis=1).astype(bf16)
    return (resid_grad, query_grad, key_grad, value_grad)


def solution(mesh):
    return jax.shard_map(
        on_device,
        mesh=mesh,
        in_specs=(
            P("ctx", None),
            P("ctx", None),
            P(),
            P("ctx", None),
            P("ctx", None),
            P(None, "exp"),
            P(None, "exp"),
            P("exp", None),
            P("exp", None),
            P("ctx", "exp"),
            P("ctx", None),
            P("ctx", None),
            P(),
        ),
        out_specs=(
            P("ctx", None),
            P("ctx", "exp"),
            P(("ctx", "exp"), None),
            P(("ctx", "exp"), None),
        ),
        check_vma=False,
    )
```

```python
import functools
import math

import jax
import jax.numpy as jnp
from jax import lax
from jax.experimental import pallas as pl
from jax.experimental.pallas import tpu as pltpu
from jax.sharding import Mesh, PartitionSpec as P

DH = 128
GROUP = 16
CAP = 16
EPS = 1e-06
LOW = -1e30
KEYS = 256
CTX = ("y", "hi", "x")
EXP = ("lo", "core")

bf16 = jnp.bfloat16
f32 = jnp.float32
SMEM = pl.BlockSpec(memory_space=pltpu.SMEM)
VMEM = pl.BlockSpec(memory_space=pltpu.VMEM)
HBM = pl.BlockSpec(memory_space=pl.ANY)


def product(left, right, left_dim=1, right_dim=0):
    return lax.dot_general(
        left, right, (((left_dim,), (right_dim,)), ((), ())), preferred_element_type=f32
    )


def params(mib):
    return pltpu.CompilerParams(vmem_limit_bytes=mib << 20)


def cost(flops, moved):
    return pl.CostEstimate(flops=flops, bytes_accessed=moved, transcendentals=0)


def shape(dims, dtype):
    return jax.ShapeDtypeStruct(dims, dtype)


def expert_kernel(
    place, ids, combine, gain, resid, out_grad, w_gate, w_up, w_down,
    give, keep, selector, resid16, grad16,
    resid_in, grad_in, gate_in, up_in, down_in, sems,
):
    copies = [
        pltpu.make_async_copy(source, target, sems.at[i])
        for i, (source, target) in enumerate(
            [(resid, resid_in), (out_grad, grad_in), (w_gate, gate_in), (w_up, up_in), (w_down, down_in)]
        )
    ]
    for copy in copies:
        copy.start()
    rows = ids.shape[1]
    hit = ids[...] == 0
    chosen_row = jnp.sum(jnp.where(hit, 1.0, 0.0), axis=0, keepdims=True)
    weight_row = jnp.sum(jnp.where(hit, combine[...], 0.0), axis=0, keepdims=True)
    before = lax.broadcasted_iota(jnp.int32, (rows, rows), 0)
    after = lax.broadcasted_iota(jnp.int32, (rows, rows), 1)
    upper = jnp.where(before <= after, 1.0, 0.0).astype(bf16)
    spread = jnp.broadcast_to(chosen_row, (CAP, rows)).astype(bf16)
    rank_row = product(spread, upper)
    slot = lax.broadcasted_iota(jnp.int32, (CAP, rows), 0).astype(f32) + 1.0
    picks = (rank_row == slot) & (chosen_row > 0.0)
    pick = jnp.where(picks, 1.0, 0.0).astype(bf16)
    selector[...] = pick
    weight16 = jnp.sum(jnp.where(picks, weight_row, 0.0), axis=1, keepdims=True)
    copies[0].wait()
    rows16 = product(pick, resid_in[...])
    resid16[...] = rows16.astype(bf16)
    rms16 = lax.rsqrt(jnp.mean(rows16 * rows16, axis=1, keepdims=True) + EPS)
    normed16 = (rows16 * rms16 * gain[...]).astype(bf16)
    copies[1].wait()
    taken = product(pick, grad_in[...])
    grad16[...] = taken.astype(bf16)
    scaled16 = (taken * weight16).astype(bf16)
    copies[2].wait()
    gate_pre = product(normed16, gate_in[...], 1, 1)
    copies[3].wait()
    up_pre = product(normed16, up_in[...], 1, 1)
    copies[4].wait()
    hidden = product(scaled16, down_in[...], 1, 1)
    sig = jax.nn.sigmoid(gate_pre)
    gate_grad = (hidden * up_pre * sig * (1.0 + gate_pre * (1.0 - sig))).astype(bf16)
    up_grad = (hidden * gate_pre * sig).astype(bf16)
    half = give.shape[1]
    first = product(gate_grad, gate_in[:, :half]) + product(up_grad, up_in[:, :half])
    second = product(gate_grad, gate_in[:, half:]) + product(up_grad, up_in[:, half:])
    low = place[1] == 0
    keep[...] = jnp.where(low, first, second)
    give[...] = jnp.where(low, second, first).astype(bf16)


def late_kernel(place, total, other, resid16, grad16, gain, w_out, rows16, late, out_in, sems):
    n = sems.shape[0]
    step = w_out.shape[0] // n
    copies = [
        pltpu.make_async_copy(
            w_out.at[pl.ds(i * step, step)], out_in.at[pl.ds(i * step, step)], sems.at[i]
        )
        for i in range(n)
    ]
    for copy in copies:
        copy.start()
    low = place[1] == 0
    first, second = total[...].astype(f32), other[...].astype(f32)
    left, right = jnp.where(low, first, second), jnp.where(low, second, first)
    gained = jnp.concatenate([left, right], axis=1) * gain[...]
    wide = resid16[...].astype(f32)
    rms = lax.rsqrt(jnp.mean(wide * wide, axis=1, keepdims=True) + EPS)
    inner = jnp.mean(gained * wide, axis=1, keepdims=True)
    done = (grad16[...].astype(f32) + rms * (gained - wide * rms * rms * inner)).astype(bf16)
    rows16[...] = done
    for i in range(n):
        copies[i].wait()
        part = product(done, out_in[i * step : (i + 1) * step], 1, 1)
        late[:, i * step : (i + 1) * step] = part.astype(bf16)


def base_kernel(w_out, out_grad, base, total):
    @pl.when(pl.program_id(0) == 0)
    def _():
        total[...] = jnp.zeros_like(total)

    total[...] += product(w_out[...], out_grad[...], 1, 1)

    @pl.when(pl.program_id(0) == pl.num_programs(0) - 1)
    def _():
        base[...] = total[...].astype(bf16)


def resid_kernel(selector, rows16, out_grad, resid_grad):
    pick = selector[...]
    chosen = product(pick, jnp.ones((CAP, 128), bf16), 0, 0)[:, :1] > 0.5
    moved = product(pick, rows16[...], 0, 0)
    resid_grad[...] = jnp.where(chosen, moved, out_grad[...].astype(f32)).astype(bf16)


def stack_heads(target, own, par):
    rows, heads = own.shape[0], own.shape[1] // DH
    for h in range(heads):
        target[h * rows : (h + 1) * rows] = own[:, h * DH : (h + 1) * DH]
        target[(h + heads) * rows : (h + heads + 1) * rows] = par[:, h * DH : (h + 1) * DH]


def forward_kernel(chunk, n_hi, n_x, place, spans, q_own, q_par, kv, weights, stats, q_all, held, top):
    phase, step = pl.program_id(0), pl.program_id(1)
    rows = q_own.shape[0]
    block = rows // 2
    columns = q_all.shape[0]
    factor = math.log2(math.e) / math.sqrt(DH)
    at = pl.ds(pl.multiple_of(step * KEYS, KEYS), KEYS)

    @pl.when((phase == 0) & (step == 0))
    def _():
        stack_heads(q_all, q_own, q_par)
        top[...] = jnp.full_like(top, 2.0 * LOW)

    @pl.when(phase == 0)
    def _():
        lane = lax.broadcasted_iota(jnp.int32, (chunk, rows), 1)
        below = lax.broadcasted_iota(jnp.int32, (chunk, rows), 0)
        here = place[0] * 2
        query_pos = jnp.where(
            lane < block, spans[here] * block + lane, spans[here + 1] * block + lane - block
        )
        per_ctx = block // chunk
        pieces = []
        for g in range(KEYS // chunk):
            held_by, i = step * (KEYS // block) + g // per_ctx, g % per_ctx
            plane, high = held_by // n_hi, held_by % n_hi
            ctx = (plane // n_x * n_hi + high) * n_x + plane % n_x
            offset = (2 * i + place[1]) * chunk
            span = spans[2 * ctx + (2 * i * chunk) // block]
            key_pos = span * block + offset % block + below
            pieces.append(jnp.where(key_pos <= query_pos, 0.0, LOW))
        bias = jnp.concatenate(pieces, axis=0)
        bias = jnp.concatenate([bias, bias], axis=1)
        key = kv[:, :DH]
        for c in range(0, columns, 2 * rows):
            score = product(key, q_all[c : c + 2 * rows], 1, 1) * factor + bias
            held[at, c : c + 2 * rows] = score
            top[:, c : c + 2 * rows] = jnp.maximum(
                top[:, c : c + 2 * rows], jnp.max(score, axis=0, keepdims=True)
            )

    @pl.when((phase == 1) & (step == 0))
    def _():
        stats[...] = jnp.zeros_like(stats)
        stats[DH : DH + 1] = top[...]

    @pl.when(phase == 1)
    def _():
        value = kv[:, DH:]
        for c in range(0, columns, 2 * rows):
            weight = jnp.exp2(held[at, c : c + 2 * rows] - top[:, c : c + 2 * rows])
            stats[DH + 1 : DH + 2, c : c + 2 * rows] += jnp.sum(weight, axis=0, keepdims=True)
            weight = weight.astype(bf16)
            weights[:, c : c + 2 * rows] = weight
            stats[:DH, c : c + 2 * rows] += product(value, weight, 0, 0)


def backward_kernel(
    q_own, q_par, base_own, base_par, late_own, late_par, selector, mine, theirs, kv, weights,
    kv_part, score_grad, q_all, grads, delta,
):
    rows, heads = q_own.shape[0], q_own.shape[1] // DH
    columns = q_all.shape[0]
    wide = heads * rows
    scale = 1.0 / math.sqrt(DH)

    @pl.when(pl.program_id(0) == 0)
    def _():
        stack_heads(q_all, q_own, q_par)
        pick = selector[...]
        chosen = jnp.sum(pick.astype(f32), axis=0, keepdims=True) > 0.5
        for side, (base, late) in enumerate([(base_own, late_own), (base_par, late_par)]):
            moved = product(late[...], pick, 0, 0)
            merged = jnp.where(chosen, moved, base[...].astype(f32))
            here, there = side * wide, (1 - side) * wide
            top, mass = mine[DH : DH + 1, here : here + wide], mine[DH + 1 : DH + 2, here : here + wide]
            far_top = theirs[DH : DH + 1, there : there + wide]
            far_mass = theirs[DH + 1 : DH + 2, there : there + wide]
            peak = jnp.maximum(top, far_top)
            near, far = jnp.exp2(top - peak), jnp.exp2(far_top - peak)
            inverse = 1.0 / (mass * near + far_mass * far)
            near, far = near * inverse, far * inverse
            out = mine[:DH, here : here + wide] * near + theirs[:DH, there : there + wide] * far
            for h in range(heads):
                part = merged[h * DH : (h + 1) * DH]
                c = slice(h * rows, (h + 1) * rows)
                to = slice(here + h * rows, here + (h + 1) * rows)
                delta[:, to] = near[:, c] * jnp.sum(part * out[:, c], axis=0, keepdims=True)
                grads[:, to] = (part * near[:, c]).astype(bf16)

    key, value = kv[:, :DH], kv[:, DH:]
    for c in range(0, columns, 2 * rows):
        prob_grad = product(value, grads[:, c : c + 2 * rows])
        weight = weights[:, c : c + 2 * rows].astype(f32)
        score_grad[:, c : c + 2 * rows] = (
            weight * (prob_grad - delta[:, c : c + 2 * rows])
        ).astype(bf16)
    kv_part[:, DH:] = product(weights[...], grads[...], 1, 1).astype(bf16)
    kv_part[:, :DH] = (product(score_grad[...], q_all[...]) * scale).astype(bf16)


def query_kernel(kv, score_grad, own, par, total):
    step = pl.program_id(0)

    @pl.when(step == 0)
    def _():
        total[...] = jnp.zeros_like(total)

    total[...] += product(kv[:, :DH], score_grad[...], 0, 0)

    @pl.when(step == pl.num_programs(0) - 1)
    def _():
        rows, heads = own.shape[0], own.shape[1] // DH
        scale = 1.0 / math.sqrt(DH)
        for h in range(heads):
            to = slice(h * DH, (h + 1) * DH)
            own[:, to] = total[:, h * rows : (h + 1) * rows].T * scale
            there = h + heads
            par[:, to] = (total[:, there * rows : (there + 1) * rows].T * scale).astype(bf16)


def across(array, axis, mask=1):
    count = lax.axis_size(axis)
    return lax.ppermute(array, axis, [(i, i ^ mask) for i in range(count)])


def on_device(
    resid, out_grad, norm_gain, expert_ids, combine, w_gate, w_up, w_down, w_out,
    queries, keys, values, span_order,
):
    rows, width = resid.shape
    heads = queries.shape[1] // DH
    hidden = w_gate.shape[1]
    n_y, n_x, n_hi, n_lo = (lax.axis_size(axis) for axis in ("y", "x", "hi", "lo"))
    exp, core, high = lax.axis_index(("lo", "core")), lax.axis_index("core"), lax.axis_index("hi")
    chunk = rows // (2 * n_lo)
    half = width // 2
    columns = 2 * heads * rows
    n_keys = n_y * n_x * n_hi * n_lo * chunk
    steps = n_keys // KEYS
    place = jnp.stack([lax.axis_index(CTX), core]).astype(jnp.int32)
    gain = norm_gain[None, :]

    kv_index = exp * heads // GROUP
    own_kv = jnp.concatenate(
        [
            lax.dynamic_slice_in_dim(keys, kv_index * DH, DH, 1),
            lax.dynamic_slice_in_dim(values, kv_index * DH, DH, 1),
        ],
        axis=1,
    ).reshape(n_lo, 2, chunk, 2 * DH)
    near_kv = jnp.where(core == 0, own_kv[:, 0], own_kv[:, 1]).reshape(n_lo * chunk, 2 * DH)
    far_kv = across(near_kv, "hi")
    plane_kv = jnp.where(
        high == 0, jnp.stack([near_kv, far_kv]), jnp.stack([far_kv, near_kv])
    )
    sent = jnp.broadcast_to(plane_kv[None], (n_y * n_x,) + plane_kv.shape)
    kv = lax.all_to_all(sent, ("y", "x"), 0, 0, tiled=True).reshape(-1, 2 * DH)
    q_par = across(queries, "core")

    give, keep, selector, resid16, grad16 = pl.pallas_call(
        expert_kernel,
        out_shape=(
            shape((CAP, half), bf16),
            shape((CAP, half), f32),
            shape((CAP, rows), bf16),
            shape((CAP, width), bf16),
            shape((CAP, width), bf16),
        ),
        in_specs=[SMEM, VMEM, VMEM, VMEM] + [HBM] * 5,
        out_specs=(VMEM,) * 5,
        scratch_shapes=[
            pltpu.VMEM((rows, width), bf16),
            pltpu.VMEM((rows, width), bf16),
            pltpu.VMEM((hidden, width), bf16),
            pltpu.VMEM((hidden, width), bf16),
            pltpu.VMEM((hidden, width), bf16),
            pltpu.SemaphoreType.DMA((5,)),
        ],
        compiler_params=params(24),
        cost_estimate=cost(10 * CAP * width * hidden, 8 << 20),
        name="expert",
    )(place, expert_ids.T, combine.T, gain, resid, out_grad, w_gate.T, w_up.T, w_down)

    pair = lax.optimization_barrier((keep + across(give, "core").astype(f32)).astype(bf16))
    r1, r2, r3 = across(pair, "lo", 1), across(pair, "lo", 2), across(pair, "lo", 3)
    total = (pair.astype(f32) + r1.astype(f32)) + (r2.astype(f32) + r3.astype(f32))
    total = lax.optimization_barrier(total.astype(bf16))
    other = across(total, "core")
    rows16, late_own = pl.pallas_call(
        late_kernel,
        out_shape=(shape((CAP, width), bf16), shape((CAP, heads * DH), bf16)),
        in_specs=[SMEM] + [VMEM] * 5 + [HBM],
        out_specs=(VMEM, VMEM),
        scratch_shapes=[
            pltpu.VMEM((heads * DH, width), bf16),
            pltpu.SemaphoreType.DMA((2,)),
        ],
        compiler_params=params(24),
        cost_estimate=cost(2 * CAP * width * heads * DH, 5 << 20),
        name="late",
    )(place, total, other, resid16, grad16, gain, w_out)
    late_par = across(late_own, "core")

    cut = 4
    base_own = pl.pallas_call(
        base_kernel,
        grid=(cut,),
        out_shape=shape((heads * DH, rows), bf16),
        in_specs=[
            pl.BlockSpec((heads * DH, width // cut), lambda i: (0, i)),
            pl.BlockSpec((rows, width // cut), lambda i: (0, i)),
        ],
        out_specs=pl.BlockSpec((heads * DH, rows), lambda i: (0, 0)),
        scratch_shapes=[pltpu.VMEM((heads * DH, rows), f32)],
        compiler_params=params(24),
        cost_estimate=cost(2 * rows * width * heads * DH, 5 << 20),
        name="base",
    )(w_out, out_grad)
    base_par = across(base_own, "core")
    resid_grad = pl.pallas_call(
        resid_kernel,
        grid=(cut,),
        out_shape=shape((rows, width), bf16),
        in_specs=[
            pl.BlockSpec((CAP, rows), lambda i: (0, 0)),
            pl.BlockSpec((CAP, width // cut), lambda i: (0, i)),
            pl.BlockSpec((rows, width // cut), lambda i: (0, i)),
        ],
        out_specs=pl.BlockSpec((rows, width // cut), lambda i: (0, i)),
        compiler_params=params(24),
        cost_estimate=cost(2 * rows * width * CAP, 2 << 20),
        name="resid",
    )(selector, rows16, out_grad)

    whole = lambda *_: (0, 0)
    query_spec = pl.BlockSpec((rows, heads * DH), whole)
    pair_flops = 2 * n_keys * columns * DH
    weights, mine = pl.pallas_call(
        functools.partial(forward_kernel, chunk, n_hi, n_x),
        grid=(2, steps),
        out_shape=(shape((n_keys, columns), bf16), shape((DH + 8, columns), f32)),
        in_specs=[
            SMEM,
            SMEM,
            query_spec,
            query_spec,
            pl.BlockSpec((KEYS, 2 * DH), lambda p, j: (j, 0)),
        ],
        out_specs=(
            pl.BlockSpec((KEYS, columns), lambda p, j: (j * p, 0)),
            pl.BlockSpec((DH + 8, columns), whole),
        ),
        scratch_shapes=[
            pltpu.VMEM((columns, DH), bf16),
            pltpu.VMEM((n_keys, columns), f32),
            pltpu.VMEM((1, columns), f32),
        ],
        compiler_params=params(24),
        cost_estimate=cost(2 * pair_flops, 6 << 20),
        name="forward",
    )(place, span_order, queries, q_par, kv)
    theirs = across(mine, "core")
    kv_part, score_grad = pl.pallas_call(
        backward_kernel,
        grid=(steps,),
        out_shape=(shape((n_keys, 2 * DH), bf16), shape((n_keys, columns), bf16)),
        in_specs=[
            query_spec,
            query_spec,
            pl.BlockSpec((heads * DH, rows), whole),
            pl.BlockSpec((heads * DH, rows), whole),
            pl.BlockSpec((CAP, heads * DH), whole),
            pl.BlockSpec((CAP, heads * DH), whole),
            pl.BlockSpec((CAP, rows), whole),
            pl.BlockSpec((DH + 8, columns), whole),
            pl.BlockSpec((DH + 8, columns), whole),
            pl.BlockSpec((KEYS, 2 * DH), lambda j: (j, 0)),
            pl.BlockSpec((KEYS, columns), lambda j: (j, 0)),
        ],
        out_specs=(
            pl.BlockSpec((KEYS, 2 * DH), lambda j: (j, 0)),
            pl.BlockSpec((KEYS, columns), lambda j: (j, 0)),
        ),
        scratch_shapes=[
            pltpu.VMEM((columns, DH), bf16),
            pltpu.VMEM((DH, columns), bf16),
            pltpu.VMEM((1, columns), f32),
        ],
        compiler_params=params(24),
        cost_estimate=cost(3 * pair_flops, 10 << 20),
        name="backward",
    )(
        queries, q_par, base_own, base_par, late_own, late_par, selector, mine, theirs, kv, weights,
    )
    got = lax.all_to_all(
        kv_part.reshape(n_y * n_x, n_hi * n_lo * chunk, 2 * DH), ("y", "x"), 0, 0, tiled=True
    )
    query_spec = pl.BlockSpec((rows, heads * DH), whole)
    query_own, query_give = pl.pallas_call(
        query_kernel,
        grid=(steps,),
        out_shape=(shape((rows, heads * DH), f32), shape((rows, heads * DH), bf16)),
        in_specs=[
            pl.BlockSpec((KEYS, 2 * DH), lambda j: (j, 0)),
            pl.BlockSpec((KEYS, columns), lambda j: (j, 0)),
        ],
        out_specs=(query_spec, query_spec),
        scratch_shapes=[pltpu.VMEM((DH, columns), f32)],
        compiler_params=params(24),
        cost_estimate=cost(pair_flops, 6 << 20),
        name="query",
    )(kv, score_grad)
    query_grad = (query_own + across(query_give, "core").astype(f32)).astype(bf16)

    owned = jnp.sum(got.astype(f32), axis=0).astype(bf16)
    owned = owned.reshape(n_hi * n_lo, chunk, 2 * DH)
    parts = lax.all_to_all(owned, ("hi", "lo"), 0, 0, tiled=True).astype(f32)
    parts = parts.reshape(n_hi, 2, n_lo // 2, chunk, 2, DH)
    summed = jnp.sum(parts, axis=(0, 2)).transpose(2, 1, 0, 3).reshape(2, chunk, 2 * DH)
    summed = summed.astype(bf16)
    key_grad, value_grad = summed[0], summed[1]
    return (resid_grad, query_grad, key_grad, value_grad)


def solution(mesh):
    fine = Mesh(mesh.devices.reshape(4, 2, 4, 4, 2), ("y", "hi", "x", "lo", "core"))
    return jax.shard_map(
        on_device,
        mesh=fine,
        in_specs=(
            P(CTX, None),
            P(CTX, None),
            P(),
            P(CTX, None),
            P(CTX, None),
            P(None, EXP),
            P(None, EXP),
            P(EXP, None),
            P(EXP, None),
            P(CTX, EXP),
            P(CTX, None),
            P(CTX, None),
            P(),
        ),
        out_specs=(
            P(CTX, None),
            P(CTX, EXP),
            P(CTX + EXP, None),
            P(CTX + EXP, None),
        ),
        check_vma=False,
    )
```

```python
import functools
import math

import jax
import jax.numpy as jnp
from jax import lax
from jax.experimental import pallas as pl
from jax.experimental.pallas import tpu as pltpu
from jax.sharding import Mesh, PartitionSpec as P

DH = 128
GROUP = 16
CAP = 16
EPS = 1e-06
LOW = -1e30
KEYS = 256
CTX = ("y", "hi", "x")
EXP = ("lh", "lb", "core")
CLIQUE = ("lb", "core")
PLANE = ("y", "x")

bf16 = jnp.bfloat16
f32 = jnp.float32
SMEM = pl.BlockSpec(memory_space=pltpu.SMEM)
VMEM = pl.BlockSpec(memory_space=pltpu.VMEM)
HBM = pl.BlockSpec(memory_space=pltpu.HBM)


def product(left, right, left_dim=1, right_dim=0):
    return lax.dot_general(
        left, right, (((left_dim,), (right_dim,)), ((), ())), preferred_element_type=f32
    )


def params(mib):
    return pltpu.CompilerParams(vmem_limit_bytes=mib << 20)


def cost(flops, moved):
    return pl.CostEstimate(flops=flops, bytes_accessed=moved, transcendentals=0)


def stay(array):
    return pltpu.with_memory_space_constraint(array, pltpu.HBM)


def shape(dims, dtype):
    return jax.ShapeDtypeStruct(dims, dtype)


def expert_kernel(
    place, ids_far, combine_far, gain_far, resid, out_grad, w_gate, w_up, w_down, w_out,
    give, keep, selector, resid16, grad16, gain, grad_in, out_in,
    ids, combine, resid_in, gate_in, up_in, down_in, sems,
):
    copies = [
        pltpu.make_async_copy(source, target, sems.at[i])
        for i, (source, target) in enumerate(
            [
                (resid, resid_in), (out_grad, grad_in), (w_gate, gate_in), (w_up, up_in),
                (w_down, down_in), (ids_far, ids), (combine_far, combine), (gain_far, gain),
                (w_out, out_in),
            ]
        )
    ]
    for copy in copies[5:8] + copies[:5] + copies[8:]:
        copy.start()
    for copy in copies[5:8]:
        copy.wait()
    rows = ids.shape[1]
    hit = ids[...] == 0
    chosen_row = jnp.sum(jnp.where(hit, 1.0, 0.0), axis=0, keepdims=True)
    weight_row = jnp.sum(jnp.where(hit, combine[...], 0.0), axis=0, keepdims=True)
    before = lax.broadcasted_iota(jnp.int32, (rows, rows), 0)
    after = lax.broadcasted_iota(jnp.int32, (rows, rows), 1)
    upper = jnp.where(before <= after, 1.0, 0.0).astype(bf16)
    spread = jnp.broadcast_to(chosen_row, (CAP, rows)).astype(bf16)
    rank_row = product(spread, upper)
    slot = lax.broadcasted_iota(jnp.int32, (CAP, rows), 0).astype(f32) + 1.0
    picks = (rank_row == slot) & (chosen_row > 0.0)
    pick = jnp.where(picks, 1.0, 0.0).astype(bf16)
    selector[...] = pick
    weight16 = jnp.sum(jnp.where(picks, weight_row, 0.0), axis=1, keepdims=True)
    copies[0].wait()
    rows16 = product(pick, resid_in[...])
    resid16[...] = rows16.astype(bf16)
    rms16 = lax.rsqrt(jnp.mean(rows16 * rows16, axis=1, keepdims=True) + EPS)
    normed16 = (rows16 * rms16 * gain[...]).astype(bf16)
    copies[1].wait()
    taken = product(pick, grad_in[...])
    grad16[...] = taken.astype(bf16)
    scaled16 = (taken * weight16).astype(bf16)
    copies[2].wait()
    gate_pre = product(normed16, gate_in[...], 1, 1)
    copies[3].wait()
    up_pre = product(normed16, up_in[...], 1, 1)
    copies[4].wait()
    hidden = product(scaled16, down_in[...], 1, 1)
    sig = jax.nn.sigmoid(gate_pre)
    gate_grad = (hidden * up_pre * sig * (1.0 + gate_pre * (1.0 - sig))).astype(bf16)
    up_grad = (hidden * gate_pre * sig).astype(bf16)
    half = give.shape[1]
    first = product(gate_grad, gate_in[:, :half]) + product(up_grad, up_in[:, :half])
    second = product(gate_grad, gate_in[:, half:]) + product(up_grad, up_in[:, half:])
    low = lax.rem(place[1], 2) == 0
    keep[...] = jnp.where(low, first, second)
    give[...] = jnp.where(low, second, first).astype(bf16)
    copies[8].wait()


def late_kernel(
    place, total, other, resid16, grad16, gain, selector, out_grad, w_out,
    resid_grad, attn_grad, merged, sem,
):
    low = lax.rem(place[1], 2) == 0
    first, second = total[...].astype(f32), other[...].astype(f32)
    left, right = jnp.where(low, first, second), jnp.where(low, second, first)
    gained = jnp.concatenate([left, right], axis=1) * gain[...]
    wide = resid16[...].astype(f32)
    rms = lax.rsqrt(jnp.mean(wide * wide, axis=1, keepdims=True) + EPS)
    inner = jnp.mean(gained * wide, axis=1, keepdims=True)
    done = (grad16[...].astype(f32) + rms * (gained - wide * rms * rms * inner)).astype(bf16)
    pick = selector[...]
    chosen = product(pick, jnp.ones((CAP, 128), bf16), 0, 0)[:, :1] > 0.5
    moved = product(pick, done, 0, 0).astype(bf16)
    merged[...] = jnp.where(chosen, moved, out_grad[...])
    copy = pltpu.make_async_copy(merged, resid_grad, sem.at[0])
    copy.start()
    attn_grad[...] = product(w_out[...], merged[...], 1, 1).astype(bf16)
    copy.wait()


def stack_heads(target, groups):
    rows, heads = groups[0].shape[0], groups[0].shape[1] // DH
    for g, group in enumerate(groups):
        for h in range(heads):
            at = (g * heads + h) * rows
            target[at : at + rows] = group[:, h * DH : (h + 1) * DH]


def forward_kernel(
    chunk, sizes, place, spans, q0, q1, q2, q3, kv, weights, out, stats, q_all, held, top
):
    phase, step = pl.program_id(0), pl.program_id(1)
    rows = q0.shape[0]
    block = rows // 2
    columns = q_all.shape[0]
    n_hi, n_x, n_lh = sizes
    factor = math.log2(math.e) / math.sqrt(DH)
    at = pl.ds(pl.multiple_of(step * KEYS, KEYS), KEYS)

    @pl.when((phase == 0) & (step == 0))
    def _():
        stack_heads(q_all, [q0, q1, q2, q3])
        top[...] = jnp.full_like(top, 2.0 * LOW)

    @pl.when(phase == 0)
    def _():
        lane = lax.broadcasted_iota(jnp.int32, (chunk, rows), 1)
        below = lax.broadcasted_iota(jnp.int32, (chunk, rows), 0)
        here = place[0] * 2
        query_pos = jnp.where(
            lane < block, spans[here] * block + lane, spans[here + 1] * block + lane - block
        )
        pieces = []
        for g in range(KEYS // chunk):
            held_by, i = step * (KEYS // chunk // n_lh) + g // n_lh, g % n_lh
            plane, high = held_by // n_hi, held_by % n_hi
            ctx = (plane // n_x * n_hi + high) * n_x + plane % n_x
            key_pos = spans[2 * ctx + i] * block + place[1] * chunk + below
            pieces.append(jnp.where(key_pos <= query_pos, 0.0, LOW))
        bias = jnp.concatenate(pieces, axis=0)
        bias = jnp.concatenate([bias, bias], axis=1)
        key = kv[:, :DH]
        for c in range(0, columns, 2 * rows):
            score = product(key, q_all[c : c + 2 * rows], 1, 1) * factor + bias
            held[at, c : c + 2 * rows] = score
            top[:, c : c + 2 * rows] = jnp.maximum(
                top[:, c : c + 2 * rows], jnp.max(score, axis=0, keepdims=True)
            )

    @pl.when((phase == 1) & (step == 0))
    def _():
        out[...] = jnp.zeros_like(out)
        stats[...] = jnp.zeros_like(stats)
        stats[0:1] = top[...]

    @pl.when(phase == 1)
    def _():
        value = kv[:, DH:]
        for c in range(0, columns, 2 * rows):
            weight = jnp.exp2(held[at, c : c + 2 * rows] - top[:, c : c + 2 * rows])
            stats[1:2, c : c + 2 * rows] += jnp.sum(weight, axis=0, keepdims=True)
            weight = weight.astype(bf16)
            weights[:, c : c + 2 * rows] = weight
            out[:, c : c + 2 * rows] += product(value, weight, 0, 0)


def merge_kernel(grad0, grad1, grad2, grad3, out, stats, grads, merged):
    rows, heads = grad0.shape[1], grad0.shape[0] // DH
    merged[...] = stats[...]
    for g, grad in enumerate([grad0, grad1, grad2, grad3]):
        for h in range(heads):
            to = slice((g * heads + h) * rows, (g * heads + h + 1) * rows)
            part = grad[h * DH : (h + 1) * DH]
            grads[:, to] = part
            merged[2:3, to] = jnp.sum(part.astype(f32) * out[:, to], axis=0, keepdims=True)


def backward_kernel(
    q0, q1, q2, q3, grads_in, stats0, stats1, stats2, stats3, kv, weights,
    kv_part, own, part1, part2, part3,
    q_all, grads, delta, score_grad, total,
):
    rows, heads = q0.shape[0], q0.shape[1] // DH
    columns = q_all.shape[0]
    wide = heads * rows
    scale = 1.0 / math.sqrt(DH)
    step = pl.program_id(0)

    @pl.when(step == 0)
    def _():
        stack_heads(q_all, [q0, q1, q2, q3])
        total[...] = jnp.zeros_like(total)
        every = [stats0, stats1, stats2, stats3]
        for g in range(len(every)):
            views = [
                stats[:, (g ^ m) * wide : (g ^ m) * wide + wide] for m, stats in enumerate(every)
            ]
            peak = functools.reduce(jnp.maximum, [view[0:1] for view in views])
            gains = [jnp.exp2(view[0:1] - peak) for view in views]
            mass = sum(view[1:2] * up for view, up in zip(views, gains))
            dots = sum(view[2:3] * up for view, up in zip(views, gains))
            inverse = 1.0 / mass
            near = gains[0] * inverse
            to = slice(g * wide, (g + 1) * wide)
            delta[:, to] = near * dots * inverse
            grads[:, to] = (grads_in[:, to].astype(f32) * near).astype(bf16)

    key, value = kv[:, :DH], kv[:, DH:]
    for c in range(0, columns, 2 * rows):
        prob_grad = product(value, grads[:, c : c + 2 * rows])
        weight = weights[:, c : c + 2 * rows].astype(f32)
        score_grad[:, c : c + 2 * rows] = (
            weight * (prob_grad - delta[:, c : c + 2 * rows])
        ).astype(bf16)
    kv_part[:, DH:] = product(weights[...], grads[...], 1, 1).astype(bf16)
    kv_part[:, :DH] = (product(score_grad[...], q_all[...]) * scale).astype(bf16)
    total[...] += product(key, score_grad[...], 0, 0)

    @pl.when(step == pl.num_programs(0) - 1)
    def _():
        for g, part in enumerate([own, part1, part2, part3]):
            for h in range(heads):
                at = (g * heads + h) * rows
                moved = total[:, at : at + rows].T * scale
                part[:, h * DH : (h + 1) * DH] = moved.astype(part.dtype)


def final_kernel(parts, key_grad, value_grad):
    n_lh = key_grad.shape[1] // DH
    for k in range(n_lh):
        summed = sum(
            parts[i].astype(f32) for i in range(k, parts.shape[0], n_lh)
        ).astype(bf16)
        key_grad[:, k * DH : (k + 1) * DH] = summed[:, :DH]
        value_grad[:, k * DH : (k + 1) * DH] = summed[:, DH:]


def across(array, axis, mask=1):
    count = lax.axis_size(axis)
    return lax.ppermute(array, axis, [(i, i ^ mask) for i in range(count)])


def shared(array):
    return [array] + [across(array, CLIQUE, mask) for mask in (1, 2, 3)]


def on_device(
    resid, out_grad, norm_gain, expert_ids, combine, w_gate, w_up, w_down, w_out,
    queries, keys, values, span_order,
):
    rows, width = resid.shape
    heads = queries.shape[1] // DH
    hidden = w_gate.shape[1]
    n_y, n_x, n_hi, n_lh, n_lb = (lax.axis_size(axis) for axis in ("y", "x", "hi", "lh", "lb"))
    core, high, share = lax.axis_index("core"), lax.axis_index("hi"), lax.axis_index(CLIQUE)
    n_share = 2 * n_lb
    chunk = rows // (n_lh * n_share)
    half = width // 2
    columns = n_share * heads * rows
    n_keys = n_y * n_x * n_hi * n_lh * chunk
    steps = n_keys // KEYS
    place = jnp.stack([lax.axis_index(CTX), share]).astype(jnp.int32)

    def chunks_of(array):
        split = array.reshape(n_lh, n_share, chunk, n_lh * DH)
        start = (0, share, 0, lax.axis_index("lh") * DH)
        return lax.dynamic_slice(split, start, (n_lh, 1, chunk, DH))[:, 0]

    own_kv = jnp.concatenate([chunks_of(keys), chunks_of(values)], axis=2)
    far_kv = across(own_kv, "hi")
    plane_kv = jnp.where(high == 0, jnp.stack([own_kv, far_kv]), jnp.stack([far_kv, own_kv]))
    sent = jnp.broadcast_to(plane_kv[None], (n_y * n_x,) + plane_kv.shape)

    give, keep, selector, resid16, grad16, gain, grad_near, out_near = pl.pallas_call(
        expert_kernel,
        out_shape=(
            shape((CAP, half), bf16),
            shape((CAP, half), f32),
            shape((CAP, rows), bf16),
            shape((CAP, width), bf16),
            shape((CAP, width), bf16),
            shape((1, width), f32),
            shape((rows, width), bf16),
            shape(w_out.shape, bf16),
        ),
        in_specs=[SMEM] + [HBM] * 9,
        out_specs=(VMEM,) * 8,
        scratch_shapes=[
            pltpu.VMEM(expert_ids.shape[::-1], jnp.int32),
            pltpu.VMEM(expert_ids.shape[::-1], f32),
            pltpu.VMEM((rows, width), bf16),
            pltpu.VMEM((hidden, width), bf16),
            pltpu.VMEM((hidden, width), bf16),
            pltpu.VMEM((hidden, width), bf16),
            pltpu.SemaphoreType.DMA((9,)),
        ],
        compiler_params=params(24),
        cost_estimate=cost(10 * CAP * width * hidden, 8 << 20),
        name="expert",
    )(
        place,
        *map(
            stay,
            (expert_ids.T, combine.T, norm_gain[None, :], resid, out_grad)
            + (w_gate.T, w_up.T, w_down, w_out),
        ),
    )

    pair = lax.optimization_barrier((keep + across(give, "core").astype(f32)).astype(bf16))
    sent, pair = lax.optimization_barrier((sent, pair))
    kv = lax.all_to_all(sent, PLANE, 0, 0, tiled=True).reshape(-1, 2 * DH)
    r1, r2, r3 = [across(pair, ("lh", "lb"), mask) for mask in (1, 2, 3)]
    total = (pair.astype(f32) + r1.astype(f32)) + (r2.astype(f32) + r3.astype(f32))
    total = lax.optimization_barrier(total.astype(bf16))
    other = across(total, "core")
    resid_grad, attn_grad = pl.pallas_call(
        late_kernel,
        out_shape=(shape((rows, width), bf16), shape((heads * DH, rows), bf16)),
        in_specs=[SMEM] + [VMEM] * 8,
        out_specs=(HBM, VMEM),
        scratch_shapes=[pltpu.VMEM((rows, width), bf16), pltpu.SemaphoreType.DMA((1,))],
        compiler_params=params(16),
        cost_estimate=cost(2 * rows * width * heads * DH, 1 << 20),
        name="late",
    )(place, total, other, resid16, grad16, gain, selector, grad_near, out_near)

    whole = lambda *_: (0, 0)
    query_spec = pl.BlockSpec((rows, heads * DH), whole)
    wide_spec = pl.BlockSpec((DH, columns), whole)
    stats_spec = pl.BlockSpec((8, columns), whole)
    query_all = shared(queries)
    pair_flops = 2 * n_keys * columns * DH
    weights, out, stats = pl.pallas_call(
        functools.partial(forward_kernel, chunk, (n_hi, n_x, n_lh)),
        grid=(2, steps),
        out_shape=(
            shape((n_keys, columns), bf16),
            shape((DH, columns), f32),
            shape((8, columns), f32),
        ),
        in_specs=[SMEM, SMEM]
        + [query_spec] * n_share
        + [pl.BlockSpec((KEYS, 2 * DH), lambda p, j: (j, 0))],
        out_specs=(
            pl.BlockSpec((KEYS, columns), lambda p, j: (j * p, 0)),
            wide_spec,
            stats_spec,
        ),
        scratch_shapes=[
            pltpu.VMEM((columns, DH), bf16),
            pltpu.VMEM((n_keys, columns), f32),
            pltpu.VMEM((1, columns), f32),
        ],
        compiler_params=params(24),
        cost_estimate=cost(2 * pair_flops, 6 << 20),
        name="forward",
    )(place, span_order, *query_all, kv)
    grads, stats = pl.pallas_call(
        merge_kernel,
        out_shape=(shape((DH, columns), bf16), shape((8, columns), f32)),
        in_specs=[VMEM] * (n_share + 2),
        out_specs=(VMEM, VMEM),
        compiler_params=params(12),
        cost_estimate=cost(2 * DH * columns, 3 << 20),
        name="merge",
    )(*shared(attn_grad), out, stats)
    kv_part, query_own, *query_give = pl.pallas_call(
        backward_kernel,
        grid=(steps,),
        out_shape=(shape((n_keys, 2 * DH), bf16), shape((rows, heads * DH), f32))
        + (shape((rows, heads * DH), bf16),) * (n_share - 1),
        in_specs=[query_spec] * n_share
        + [wide_spec]
        + [stats_spec] * n_share
        + [
            pl.BlockSpec((KEYS, 2 * DH), lambda j: (j, 0)),
            pl.BlockSpec((KEYS, columns), lambda j: (j, 0)),
        ],
        out_specs=(pl.BlockSpec((KEYS, 2 * DH), lambda j: (j, 0)),) + (query_spec,) * n_share,
        scratch_shapes=[
            pltpu.VMEM((columns, DH), bf16),
            pltpu.VMEM((DH, columns), bf16),
            pltpu.VMEM((1, columns), f32),
            pltpu.VMEM((KEYS, columns), bf16),
            pltpu.VMEM((DH, columns), f32),
        ],
        compiler_params=params(24),
        cost_estimate=cost(4 * pair_flops, 8 << 20),
        name="backward",
    )(*query_all, grads, *shared(stats), kv, weights)
    got = lax.all_to_all(
        kv_part.reshape(n_y * n_x, n_hi * n_lh * chunk, 2 * DH), PLANE, 0, 0, tiled=True
    )
    query_parts = [
        across(part, CLIQUE, mask).astype(f32) for mask, part in enumerate(query_give, 1)
    ]
    query_grad = (query_own + sum(query_parts)).astype(bf16)

    owned = jnp.sum(got.astype(f32), axis=0).astype(bf16)
    owned = owned.reshape(n_hi * n_lh, chunk, 2 * DH)
    parts = lax.all_to_all(owned, ("hi", "lh"), 0, 0, tiled=True)
    key_grad, value_grad = pl.pallas_call(
        final_kernel,
        out_shape=(shape((chunk, n_lh * DH), bf16),) * 2,
        in_specs=[VMEM],
        out_specs=(VMEM, VMEM),
        compiler_params=params(8),
        name="final",
    )(parts)
    return (resid_grad, query_grad, key_grad, value_grad)


def solution(mesh):
    fine = Mesh(mesh.devices.reshape(4, 2, 4, 2, 2, 2), CTX + EXP)
    return jax.shard_map(
        on_device,
        mesh=fine,
        in_specs=(
            P(CTX, None),
            P(CTX, None),
            P(),
            P(CTX, None),
            P(CTX, None),
            P(None, EXP),
            P(None, EXP),
            P(EXP, None),
            P(EXP, None),
            P(CTX, EXP),
            P(CTX, None),
            P(CTX, None),
            P(),
        ),
        out_specs=(
            P(CTX, None),
            P(CTX, EXP),
            P(CTX + EXP, None),
            P(CTX + EXP, None),
        ),
        check_vma=False,
    )
```

```python
import functools
import itertools
import math

import jax
import jax.numpy as jnp
from jax import lax
from jax.experimental import pallas as pl
from jax.experimental.pallas import tpu as pltpu
from jax.sharding import Mesh, PartitionSpec as P

DH = 128
GROUP = 16
CAP = 16
EPS = 1e-06
LOW = -1e30
AHEAD = 4
CTX = ("y", "hi", "x")
EXP = ("lh", "lb", "core")
CLIQUE = ("lb", "core")
PLANE = ("y", "x")
RING = (0, 1, 2, 3)

bf16 = jnp.bfloat16
f32 = jnp.float32
SMEM = pl.BlockSpec(memory_space=pltpu.SMEM)
VMEM = pl.BlockSpec(memory_space=pltpu.VMEM)
HBM = pl.BlockSpec(memory_space=pltpu.HBM)


def product(left, right, left_dim=1, right_dim=0):
    return lax.dot_general(
        left, right, (((left_dim,), (right_dim,)), ((), ())), preferred_element_type=f32
    )


def params(mib):
    return pltpu.CompilerParams(vmem_limit_bytes=mib << 20)


def cost(flops, moved):
    return pl.CostEstimate(flops=flops, bytes_accessed=moved, transcendentals=0)


def stay(array):
    return pltpu.with_memory_space_constraint(array, pltpu.HBM)


def shape(dims, dtype):
    return jax.ShapeDtypeStruct(dims, dtype)


def expert_kernel(
    flags, ids_far, combine_far, gain_far, resid, out_grad, w_gate, w_up, w_down,
    give, keep, selector, resid16, grad16, gain,
    ids, combine, resid_in, grad_in, wide_in, down_in, sems,
):
    hidden_rows = w_down.shape[0]
    cuts = (sems.shape[0] - 5) // 3
    step = w_down.shape[1] // cuts
    heads = [
        pltpu.make_async_copy(source, target, sems.at[i])
        for i, (source, target) in enumerate(
            [
                (ids_far, ids),
                (combine_far, combine),
                (gain_far, gain),
                (resid, resid_in),
                (out_grad, grad_in),
            ]
        )
    ]
    spans = [pl.ds(i * step, step) for i in range(cuts)]
    bodies = [
        [
            pltpu.make_async_copy(
                source.at[:, span], target.at[pl.ds(row, hidden_rows), span], sems.at[5 + 3 * i + j]
            )
            for j, (source, target, row) in enumerate(
                [(w_gate, wide_in, 0), (w_up, wide_in, hidden_rows), (w_down, down_in, 0)]
            )
        ]
        for i, span in enumerate(spans)
    ]
    for copy in heads:
        copy.start()
    for body in bodies[:AHEAD]:
        for copy in body:
            copy.start()
    for copy in heads[:3]:
        copy.wait()
    rows = ids.shape[1]
    hit = ids[...] == 0
    chosen_row = jnp.sum(jnp.where(hit, 1.0, 0.0), axis=0, keepdims=True)
    weight_row = jnp.sum(jnp.where(hit, combine[...], 0.0), axis=0, keepdims=True)
    before = lax.broadcasted_iota(jnp.int32, (rows, rows), 0)
    after = lax.broadcasted_iota(jnp.int32, (rows, rows), 1)
    upper = jnp.where(before <= after, 1.0, 0.0).astype(bf16)
    spread = jnp.broadcast_to(chosen_row, (CAP, rows)).astype(bf16)
    rank_row = product(spread, upper)
    slot = lax.broadcasted_iota(jnp.int32, (CAP, rows), 0).astype(f32) + 1.0
    picks = (rank_row == slot) & (chosen_row > 0.0)
    pick = jnp.where(picks, 1.0, 0.0).astype(bf16)
    selector[...] = pick
    weight16 = jnp.sum(jnp.where(picks, weight_row, 0.0), axis=1, keepdims=True)
    heads[3].wait()
    rows16 = product(pick, resid_in[...])
    resid16[...] = rows16.astype(bf16)
    rms16 = lax.rsqrt(jnp.mean(rows16 * rows16, axis=1, keepdims=True) + EPS)
    normed16 = (rows16 * rms16 * gain[...]).astype(bf16)
    heads[4].wait()
    taken = product(pick, grad_in[...])
    grad16[...] = taken.astype(bf16)
    scaled16 = (taken * weight16).astype(bf16)
    pre = hidden = 0.0
    for i, span in enumerate(spans):
        for copy in bodies[i]:
            copy.wait()
        if i + AHEAD < cuts:
            for copy in bodies[i + AHEAD]:
                copy.start()
        at = slice(i * step, (i + 1) * step)
        pre += product(normed16[:, at], wide_in[:, span], 1, 1)
        hidden += product(scaled16[:, at], down_in[:, span], 1, 1)
    pre, hidden = pre.T, hidden.T
    gate_pre, up_pre = pre[:hidden_rows], pre[hidden_rows:]
    sig = jax.nn.sigmoid(gate_pre)
    gate_grad = hidden * up_pre * sig * (1.0 + gate_pre * (1.0 - sig))
    up_grad = hidden * gate_pre * sig
    both = jnp.concatenate([gate_grad, up_grad], axis=0).astype(bf16)
    half = give.shape[1]
    first = product(both, wide_in[:, :half], 0, 0)
    second = product(both, wide_in[:, half:], 0, 0)
    low = flags[0:1, 0:1] == 0.0
    keep[...] = jnp.where(low, first, second)
    give[...] = jnp.where(low, second, first).astype(bf16)


def late_kernel(
    flags, summed, other, resid16, grad16, gain, selector, out_grad, w_out,
    resid_grad, attn_grad, merged, grad_in, out_in, sems,
):
    cuts = sems.shape[0] - 2
    step = w_out.shape[1] // cuts
    arrive = pltpu.make_async_copy(out_grad, grad_in, sems.at[cuts])
    arrive.start()
    spans = [pl.ds(i * step, step) for i in range(cuts)]
    copies = [
        pltpu.make_async_copy(w_out.at[:, span], out_in.at[:, span], sems.at[i])
        for i, span in enumerate(spans)
    ]
    for copy in copies[:AHEAD]:
        copy.start()
    low = flags[0:1, 0:1] == 0.0
    first, second = summed[...].astype(f32), other[...].astype(f32)
    left, right = jnp.where(low, first, second), jnp.where(low, second, first)
    gained = jnp.concatenate([left, right], axis=1) * gain[...]
    wide = resid16[...].astype(f32)
    rms = lax.rsqrt(jnp.mean(wide * wide, axis=1, keepdims=True) + EPS)
    inner = jnp.mean(gained * wide, axis=1, keepdims=True)
    done = (grad16[...].astype(f32) + rms * (gained - wide * rms * rms * inner)).astype(bf16)
    pick = selector[...]
    chosen = product(pick, jnp.ones((CAP, 128), bf16), 0, 0)[:, :1] > 0.5
    moved = product(pick, done, 0, 0).astype(bf16)
    arrive.wait()
    merged[...] = jnp.where(chosen, moved, grad_in[...])
    leave = pltpu.make_async_copy(merged, resid_grad, sems.at[cuts + 1])
    leave.start()
    total = 0.0
    for i, span in enumerate(spans):
        copies[i].wait()
        if i + AHEAD < cuts:
            copies[i + AHEAD].start()
        total += product(out_in[:, span], merged[:, span], 1, 1)
    attn_grad[...] = total.astype(bf16)
    leave.wait()


def stack_heads(target, groups):
    rows, heads = groups[0].shape[0], groups[0].shape[1] // DH
    for g, group in enumerate(groups):
        for h in range(heads):
            at = (g * heads + h) * rows
            target[at : at + rows] = group[:, h * DH : (h + 1) * DH]


def forward_kernel(
    chunk, order, place, spans, q0, q1, q2, q3, kv, weights, out, stats, q_all, held, top
):
    phase = pl.program_id(0)
    rows = q0.shape[0]
    block = rows // 2
    columns = q_all.shape[0]
    factor = math.log2(math.e) / math.sqrt(DH)

    @pl.when(phase == 0)
    def _():
        stack_heads(q_all, [q0, q1, q2, q3])
        top[...] = jnp.full_like(top, 2.0 * LOW)

    @pl.when(phase == 0)
    def _():
        lane = lax.broadcasted_iota(jnp.int32, (chunk, rows), 1)
        below = lax.broadcasted_iota(jnp.int32, (chunk, rows), 0)
        here = place[0] * 2
        query_pos = jnp.where(
            lane < block, spans[here] * block + lane, spans[here + 1] * block + lane - block
        )
        pieces = []
        for ctx, i in order:
            key_pos = spans[2 * ctx + i] * block + place[1] * chunk + below
            pieces.append(jnp.where(key_pos <= query_pos, 0.0, LOW))
        bias = jnp.concatenate(pieces, axis=0)
        bias = jnp.concatenate([bias, bias], axis=1)
        key = kv[:, :DH]
        for c in range(0, columns, 2 * rows):
            score = product(key, q_all[c : c + 2 * rows], 1, 1) * factor + bias
            held[:, c : c + 2 * rows] = score
            top[:, c : c + 2 * rows] = jnp.maximum(
                top[:, c : c + 2 * rows], jnp.max(score, axis=0, keepdims=True)
            )

    @pl.when(phase == 1)
    def _():
        out[...] = jnp.zeros_like(out)
        stats[...] = jnp.zeros_like(stats)
        stats[0:1] = top[...]

    @pl.when(phase == 1)
    def _():
        value = kv[:, DH:]
        for c in range(0, columns, 2 * rows):
            weight = jnp.exp2(held[:, c : c + 2 * rows] - top[:, c : c + 2 * rows])
            stats[1:2, c : c + 2 * rows] += jnp.sum(weight, axis=0, keepdims=True)
            weight = weight.astype(bf16)
            weights[:, c : c + 2 * rows] = weight
            out[:, c : c + 2 * rows] += product(value, weight, 0, 0)


def merge_kernel(grad0, grad1, grad2, grad3, out, stats, grads, packed):
    rows, heads = grad0.shape[1], grad0.shape[0] // DH
    wide = packed.shape[1] // 3
    for g, grad in enumerate([grad0, grad1, grad2, grad3]):
        for h in range(heads):
            at = (g * heads + h) * rows
            to = slice(at, at + rows)
            part = grad[h * DH : (h + 1) * DH]
            grads[:, to] = part
            row, column = at // wide, at % wide
            for k, value in enumerate(
                [stats[0:1, to], stats[1:2, to], jnp.sum(part.astype(f32) * out[:, to], axis=0, keepdims=True)]
            ):
                packed[row : row + 1, k * wide + column : k * wide + column + rows] = value


def backward_kernel(
    order, q0, q1, q2, q3, grads_in, stats0, stats1, stats2, stats3, kv, weights,
    kv_part, own, part1, part2, part3,
    q_all, grads, delta, score_grad,
):
    rows, heads = q0.shape[0], q0.shape[1] // DH
    columns = q_all.shape[0]
    wide = heads * rows
    scale = 1.0 / math.sqrt(DH)
    stack_heads(q_all, [q0, q1, q2, q3])
    every = [stats0, stats1, stats2, stats3]
    lanes = stats0.shape[1] // 3
    each = wide // lanes
    for g in range(len(every)):
        views = [stats[(g ^ m) * each : (g ^ m) * each + each] for m, stats in enumerate(every)]
        tops = [view[:, :lanes] for view in views]
        peak = functools.reduce(jnp.maximum, tops)
        gains = [jnp.exp2(top - peak) for top in tops]
        mass = sum(view[:, lanes : 2 * lanes] * up for view, up in zip(views, gains))
        dots = sum(view[:, 2 * lanes :] * up for view, up in zip(views, gains))
        inverse = 1.0 / mass
        near = gains[0] * inverse
        middle = near * dots * inverse
        for r in range(each):
            to = slice(g * wide + r * lanes, g * wide + (r + 1) * lanes)
            delta[:, to] = middle[r : r + 1]
            grads[:, to] = (grads_in[:, to].astype(f32) * near[r : r + 1]).astype(bf16)

    key, value = kv[:, :DH], kv[:, DH:]
    for c in range(0, columns, 2 * rows):
        at = slice(c, c + 2 * rows)
        prob_grad = product(value, grads[:, at])
        score_grad[:, at] = (weights[:, at].astype(f32) * (prob_grad - delta[:, at])).astype(bf16)
    value_part = product(weights[...], grads[...], 1, 1).astype(bf16)
    key_part = (product(score_grad[...], q_all[...]) * scale).astype(bf16)
    group = key.shape[0] // len(order)
    for g, to in enumerate(order):
        at, to = slice(g * group, (g + 1) * group), slice(to * group, (to + 1) * group)
        kv_part[to, :DH] = key_part[at]
        kv_part[to, DH:] = value_part[at]
    for g, part in enumerate([own, part1, part2, part3]):
        total = product(key, score_grad[:, g * wide : (g + 1) * wide], 0, 0)
        for h in range(heads):
            moved = total[:, h * rows : (h + 1) * rows].T * scale
            part[:, h * DH : (h + 1) * DH] = moved.astype(part.dtype)


def final_kernel(flags, own, lower, upper, both, key_grad, value_grad):
    same = own[...].astype(f32) + upper[...].astype(f32)
    rest = lower[...].astype(f32) + both[...].astype(f32)
    low = flags[1:2, 0:1] == 0.0
    first, second = jnp.where(low, same, rest), jnp.where(low, rest, same)
    for k, summed in enumerate([first, second]):
        key_grad[:, k * DH : (k + 1) * DH] = summed[:, :DH].astype(bf16)
        value_grad[:, k * DH : (k + 1) * DH] = summed[:, DH:].astype(bf16)


def across(array, axis, mask=1):
    count = lax.axis_size(axis)
    return lax.ppermute(array, axis, [(i, i ^ mask) for i in range(count)])


def shared(array):
    return [array] + [across(array, CLIQUE, mask) for mask in (1, 2, 3)]


def on_device(
    resid, out_grad, norm_gain, expert_ids, combine, w_gate, w_up, w_down, w_out,
    queries, keys, values, span_order,
):
    rows, width = resid.shape
    heads = queries.shape[1] // DH
    hidden = w_gate.shape[1]
    n_y, n_x, n_hi, n_lh, n_lb = (lax.axis_size(axis) for axis in ("y", "x", "hi", "lh", "lb"))
    core, high, share = lax.axis_index("core"), lax.axis_index("hi"), lax.axis_index(CLIQUE)
    n_share = 2 * n_lb
    chunk = rows // (n_lh * n_share)
    half = width // 2
    columns = n_share * heads * rows
    n_keys = n_y * n_x * n_hi * n_lh * chunk
    place = jnp.stack([lax.axis_index(CTX), share]).astype(jnp.int32)
    group = lax.axis_index("lh")
    flags = jnp.where(lax.broadcasted_iota(jnp.int32, (8, 128), 0) == 0, core, group).astype(f32)

    def chunks_of(array, head):
        split = array.reshape(n_lh, n_share, chunk, n_lh * DH)
        start = (0, share, 0, head * DH)
        return lax.dynamic_slice(split, start, (n_lh, 1, chunk, DH))[:, 0]

    def both_of(head):
        return jnp.concatenate([chunks_of(keys, head), chunks_of(values, head)], axis=2)

    give, keep, selector, resid16, grad16, gain = pl.pallas_call(
        expert_kernel,
        out_shape=(
            shape((CAP, half), bf16),
            shape((CAP, half), f32),
            shape((CAP, rows), bf16),
            shape((CAP, width), bf16),
            shape((CAP, width), bf16),
            shape((1, width), f32),
        ),
        in_specs=[VMEM] + [HBM] * 8,
        out_specs=(VMEM,) * 6,
        scratch_shapes=[
            pltpu.VMEM(expert_ids.shape[::-1], jnp.int32),
            pltpu.VMEM(expert_ids.shape[::-1], f32),
            pltpu.VMEM((rows, width), bf16),
            pltpu.VMEM((rows, width), bf16),
            pltpu.VMEM((2 * hidden, width), bf16),
            pltpu.VMEM((hidden, width), bf16),
            pltpu.SemaphoreType.DMA((17,)),
        ],
        compiler_params=params(24),
        cost_estimate=cost(10 * CAP * width * hidden, 8 << 20),
        name="expert",
    )(
        flags,
        *map(
            stay,
            (expert_ids.T, combine.T, norm_gain[None, :], resid, out_grad)
            + (w_gate.T, w_up.T, w_down),
        ),
    )

    own_kv = both_of(group)
    leaving, give = lax.optimization_barrier((both_of(1 - group), give))
    far_kv = across(leaving, ("hi", "lh"), 3)
    plane_kv = jnp.where(high == 0, jnp.stack([own_kv, far_kv]), jnp.stack([far_kv, own_kv]))
    sent = jnp.broadcast_to(plane_kv[None], (n_y * n_x,) + plane_kv.shape)

    pair = lax.optimization_barrier((keep + across(give, "core").astype(f32)).astype(bf16))
    kv = lax.all_to_all(sent, PLANE, 0, 0, tiled=True).reshape(-1, 2 * DH)
    r1, r2, r3 = [across(pair, ("lh", "lb"), mask) for mask in (1, 2, 3)]
    total = (pair.astype(f32) + r1.astype(f32)) + (r2.astype(f32) + r3.astype(f32))
    total = lax.optimization_barrier(total.astype(bf16))
    other = across(total, "core")
    resid_grad, attn_grad = pl.pallas_call(
        late_kernel,
        out_shape=(shape((rows, width), bf16), shape((heads * DH, rows), bf16)),
        in_specs=[VMEM] * 7 + [HBM] * 2,
        out_specs=(HBM, VMEM),
        scratch_shapes=[
            pltpu.VMEM((rows, width), bf16),
            pltpu.VMEM((rows, width), bf16),
            pltpu.VMEM(w_out.shape, bf16),
            pltpu.SemaphoreType.DMA((4,)),
        ],
        compiler_params=params(16),
        cost_estimate=cost(1 << 20, 1 << 16),
        name="late",
    )(flags, total, other, resid16, grad16, gain, selector, stay(out_grad), stay(w_out))

    query_all = shared(queries)
    tour = list(itertools.product(RING, RING))
    places = [y * n_x + x for y, x in tour]
    held = [
        ((y * n_hi + hi) * n_x + x, i) for y, x in tour for hi in range(n_hi) for i in range(n_lh)
    ]
    whole = lambda *_: (0, 0)
    pair_flops = 2 * n_keys * columns * DH
    weights, out, stats = pl.pallas_call(
        functools.partial(forward_kernel, chunk, held),
        grid=(2,),
        out_shape=(
            shape((n_keys, columns), bf16),
            shape((DH, columns), f32),
            shape((8, columns), f32),
        ),
        in_specs=[SMEM, SMEM] + [pl.BlockSpec((rows, heads * DH), whole)] * n_share
        + [pl.BlockSpec((n_keys, 2 * DH), whole)],
        out_specs=(
            pl.BlockSpec((n_keys, columns), whole),
            pl.BlockSpec((DH, columns), whole),
            pl.BlockSpec((8, columns), whole),
        ),
        scratch_shapes=[
            pltpu.VMEM((columns, DH), bf16),
            pltpu.VMEM((n_keys, columns), f32),
            pltpu.VMEM((1, columns), f32),
        ],
        compiler_params=params(24),
        cost_estimate=cost(2 * pair_flops, 6 << 20),
        name="forward",
    )(place, span_order, *query_all, kv)
    grads, packed = pl.pallas_call(
        merge_kernel,
        out_shape=(shape((DH, columns), bf16), shape((8, 3 * columns // 8), f32)),
        in_specs=[VMEM] * (n_share + 2),
        out_specs=(VMEM, VMEM),
        compiler_params=params(12),
        cost_estimate=cost(2 * DH * columns, 3 << 20),
        name="merge",
    )(*shared(attn_grad), out, stats)
    kv_part, query_own, *query_give = pl.pallas_call(
        functools.partial(backward_kernel, places),
        out_shape=(shape((n_keys, 2 * DH), bf16), shape((rows, heads * DH), f32))
        + (shape((rows, heads * DH), bf16),) * (n_share - 1),
        in_specs=[VMEM] * (2 * n_share + 3),
        out_specs=(VMEM,) * (n_share + 1),
        scratch_shapes=[
            pltpu.VMEM((columns, DH), bf16),
            pltpu.VMEM((DH, columns), bf16),
            pltpu.VMEM((1, columns), f32),
            pltpu.VMEM((n_keys, columns), bf16),
        ],
        compiler_params=params(16),
        cost_estimate=cost(4 * pair_flops, 8 << 20),
        name="backward",
    )(*query_all, grads, *shared(packed), kv, weights)
    got = lax.all_to_all(
        kv_part.reshape(n_y * n_x, n_hi * n_lh * chunk, 2 * DH), PLANE, 0, 0, tiled=True
    )
    query_parts = [
        across(part, CLIQUE, mask).astype(f32) for mask, part in enumerate(query_give, 1)
    ]
    query_grad = (query_own + sum(query_parts)).astype(bf16)

    owned = jnp.sum(got.astype(f32), axis=0).astype(bf16)
    owned = owned.reshape(n_hi * n_lh, chunk, 2 * DH)
    here = 2 * high + group
    parts = [lax.dynamic_index_in_dim(owned, here, 0, keepdims=False)] + [
        across(lax.dynamic_index_in_dim(owned, here ^ mask, 0, keepdims=False), ("hi", "lh"), mask)
        for mask in (1, 2, 3)
    ]
    key_grad, value_grad = pl.pallas_call(
        final_kernel,
        out_shape=(shape((chunk, n_lh * DH), bf16),) * 2,
        in_specs=[VMEM] * 5,
        out_specs=(VMEM, VMEM),
        compiler_params=params(8),
        name="final",
    )(flags, *parts)
    return (resid_grad, query_grad, key_grad, value_grad)


def solution(mesh):
    fine = Mesh(mesh.devices.reshape(4, 2, 4, 2, 2, 2), CTX + EXP)
    return jax.shard_map(
        on_device,
        mesh=fine,
        in_specs=(
            P(CTX, None),
            P(CTX, None),
            P(),
            P(CTX, None),
            P(CTX, None),
            P(None, EXP),
            P(None, EXP),
            P(EXP, None),
            P(EXP, None),
            P(CTX, EXP),
            P(CTX, None),
            P(CTX, None),
            P(),
        ),
        out_specs=(
            P(CTX, None),
            P(CTX, EXP),
            P(CTX + EXP, None),
            P(CTX + EXP, None),
        ),
        check_vma=False,
    )
```

```python
import functools
import itertools
import math

import jax
import jax.numpy as jnp
from jax import lax
from jax.experimental import pallas as pl
from jax.experimental.pallas import tpu as pltpu
from jax.sharding import Mesh, PartitionSpec as P

DH = 128
GROUP = 16
CAP = 16
EPS = 1e-06
LOW = -1e30
AHEAD = 4
CTX = ("y", "hi", "x")
EXP = ("lh", "lb", "core")
CLIQUE = ("lb", "core")
PLANE = ("y", "x")

bf16 = jnp.bfloat16
f32 = jnp.float32
SMEM = pl.BlockSpec(memory_space=pltpu.SMEM)
VMEM = pl.BlockSpec(memory_space=pltpu.VMEM)
HBM = pl.BlockSpec(memory_space=pltpu.HBM)


def product(left, right, left_dim=1, right_dim=0):
    return lax.dot_general(
        left, right, (((left_dim,), (right_dim,)), ((), ())), preferred_element_type=f32
    )


def params(mib):
    return pltpu.CompilerParams(vmem_limit_bytes=mib << 20)


def cost(flops, moved):
    return pl.CostEstimate(flops=flops, bytes_accessed=moved, transcendentals=0)


def stay(array):
    return pltpu.with_memory_space_constraint(array, pltpu.HBM)


def shape(dims, dtype):
    return jax.ShapeDtypeStruct(dims, dtype)


def expert_kernel(
    flags, ids_far, combine_far, gain_far, resid, out_grad, w_gate, w_up, w_down,
    keys, values, give, keep, selector, resid16, grad16, gain, own_kv, leaving_kv,
    ids, combine, resid_in, grad_in, wide_in, down_in, keys_in, values_in, sems,
):
    hidden_rows = w_down.shape[0]
    cuts = (sems.shape[0] - 7) // 3
    step = w_down.shape[1] // cuts
    heads = [
        pltpu.make_async_copy(source, target, sems.at[i])
        for i, (source, target) in enumerate(
            [
                (ids_far, ids),
                (combine_far, combine),
                (gain_far, gain),
                (resid, resid_in),
                (out_grad, grad_in),
                (keys, keys_in),
                (values, values_in),
            ]
        )
    ]
    spans = [pl.ds(i * step, step) for i in range(cuts)]
    bodies = [
        [
            pltpu.make_async_copy(
                source.at[:, span], target.at[pl.ds(row, hidden_rows), span], sems.at[7 + 3 * i + j]
            )
            for j, (source, target, row) in enumerate(
                [(w_gate, wide_in, 0), (w_up, wide_in, hidden_rows), (w_down, down_in, 0)]
            )
        ]
        for i, span in enumerate(spans)
    ]
    for copy in heads:
        copy.start()
    for body in bodies[:AHEAD]:
        for copy in body:
            copy.start()
    for copy in heads[:3] + heads[5:]:
        copy.wait()
    core, high_head, upper_pair = [flags[i : i + 1, 0:1] > 0.5 for i in range(3)]
    chunk = own_kv.shape[1]
    for i in range(own_kv.shape[0]):
        for side, source in enumerate((keys_in, values_in)):
            p = [source[(4 * i + k) * chunk : (4 * i + k + 1) * chunk] for k in range(4)]
            mine = jnp.where(upper_pair, jnp.where(core, p[3], p[2]), jnp.where(core, p[1], p[0]))
            left, right = mine[:, :DH], mine[:, DH:]
            to = slice(side * DH, (side + 1) * DH)
            own_kv[i, :, to] = jnp.where(high_head, right, left)
            leaving_kv[i, :, to] = jnp.where(high_head, left, right)
    rows = ids.shape[1]
    hit = ids[...] == 0
    chosen_row = jnp.sum(jnp.where(hit, 1.0, 0.0), axis=0, keepdims=True)
    weight_row = jnp.sum(jnp.where(hit, combine[...], 0.0), axis=0, keepdims=True)
    before = lax.broadcasted_iota(jnp.int32, (rows, rows), 0)
    after = lax.broadcasted_iota(jnp.int32, (rows, rows), 1)
    upper = jnp.where(before <= after, 1.0, 0.0).astype(bf16)
    spread = jnp.broadcast_to(chosen_row, (CAP, rows)).astype(bf16)
    rank_row = product(spread, upper)
    slot = lax.broadcasted_iota(jnp.int32, (CAP, rows), 0).astype(f32) + 1.0
    picks = (rank_row == slot) & (chosen_row > 0.0)
    pick = jnp.where(picks, 1.0, 0.0).astype(bf16)
    selector[...] = pick
    weight16 = jnp.sum(jnp.where(picks, weight_row, 0.0), axis=1, keepdims=True)
    heads[3].wait()
    rows16 = product(pick, resid_in[...])
    resid16[...] = rows16.astype(bf16)
    rms16 = lax.rsqrt(jnp.mean(rows16 * rows16, axis=1, keepdims=True) + EPS)
    normed16 = (rows16 * rms16 * gain[...]).astype(bf16)
    heads[4].wait()
    taken = product(pick, grad_in[...])
    grad16[...] = taken.astype(bf16)
    scaled16 = (taken * weight16).astype(bf16)
    pre = hidden = 0.0
    for i, span in enumerate(spans):
        for copy in bodies[i]:
            copy.wait()
        if i + AHEAD < cuts:
            for copy in bodies[i + AHEAD]:
                copy.start()
        at = slice(i * step, (i + 1) * step)
        pre += product(normed16[:, at], wide_in[:, span], 1, 1)
        hidden += product(scaled16[:, at], down_in[:, span], 1, 1)
    pre, hidden = pre.T, hidden.T
    gate_pre, up_pre = pre[:hidden_rows], pre[hidden_rows:]
    sig = jax.nn.sigmoid(gate_pre)
    gate_grad = hidden * up_pre * sig * (1.0 + gate_pre * (1.0 - sig))
    up_grad = hidden * gate_pre * sig
    both = jnp.concatenate([gate_grad, up_grad], axis=0).astype(bf16)
    half = give.shape[1]
    first = product(both, wide_in[:, :half], 0, 0)
    second = product(both, wide_in[:, half:], 0, 0)
    low = flags[0:1, 0:1] == 0.0
    keep[...] = jnp.where(low, first, second)
    give[...] = jnp.where(low, second, first).astype(bf16)


def late_kernel(
    flags, summed, other, resid16, grad16, gain, selector, out_grad, w_out,
    resid_grad, attn_grad, merged, grad_in, out_in, sems,
):
    cuts = sems.shape[0] - 2
    step = w_out.shape[1] // cuts
    arrive = pltpu.make_async_copy(out_grad, grad_in, sems.at[cuts])
    arrive.start()
    spans = [pl.ds(i * step, step) for i in range(cuts)]
    copies = [
        pltpu.make_async_copy(w_out.at[:, span], out_in.at[:, span], sems.at[i])
        for i, span in enumerate(spans)
    ]
    for copy in copies[:AHEAD]:
        copy.start()
    low = flags[0:1, 0:1] == 0.0
    first, second = summed[...].astype(f32), other[...].astype(f32)
    left, right = jnp.where(low, first, second), jnp.where(low, second, first)
    gained = jnp.concatenate([left, right], axis=1) * gain[...]
    wide = resid16[...].astype(f32)
    rms = lax.rsqrt(jnp.mean(wide * wide, axis=1, keepdims=True) + EPS)
    inner = jnp.mean(gained * wide, axis=1, keepdims=True)
    done = (grad16[...].astype(f32) + rms * (gained - wide * rms * rms * inner)).astype(bf16)
    pick = selector[...]
    chosen = product(pick, jnp.ones((CAP, 128), bf16), 0, 0)[:, :1] > 0.5
    moved = product(pick, done, 0, 0).astype(bf16)
    arrive.wait()
    merged[...] = jnp.where(chosen, moved, grad_in[...])
    leave = pltpu.make_async_copy(merged, resid_grad, sems.at[cuts + 1])
    leave.start()
    total = 0.0
    for i, span in enumerate(spans):
        copies[i].wait()
        if i + AHEAD < cuts:
            copies[i + AHEAD].start()
        total += product(out_in[:, span], merged[:, span], 1, 1)
    attn_grad[...] = total.astype(bf16)
    leave.wait()


def stack_heads(target, groups):
    rows, heads = groups[0].shape[0], groups[0].shape[1] // DH
    for g, group in enumerate(groups):
        for h in range(heads):
            at = (g * heads + h) * rows
            target[at : at + rows] = group[:, h * DH : (h + 1) * DH]


def forward_kernel(
    chunk, order, place, spans, q0, q1, q2, q3, kv, weights, out, stats, q_all, held, top
):
    phase = pl.program_id(0)
    rows = q0.shape[0]
    block = rows // 2
    columns = q_all.shape[0]
    factor = math.log2(math.e) / math.sqrt(DH)

    @pl.when(phase == 0)
    def _():
        stack_heads(q_all, [q0, q1, q2, q3])
        top[...] = jnp.full_like(top, 2.0 * LOW)

    @pl.when(phase == 0)
    def _():
        lane = lax.broadcasted_iota(jnp.int32, (chunk, rows), 1)
        below = lax.broadcasted_iota(jnp.int32, (chunk, rows), 0)
        here = place[0] * 2
        query_pos = jnp.where(
            lane < block, spans[here] * block + lane, spans[here + 1] * block + lane - block
        )
        pieces = []
        for ctx, i in order:
            key_pos = spans[2 * ctx + i] * block + place[1] * chunk + below
            pieces.append(jnp.where(key_pos <= query_pos, 0.0, LOW))
        bias = jnp.concatenate(pieces, axis=0)
        bias = jnp.concatenate([bias, bias], axis=1)
        key = kv[:, :DH]
        for c in range(0, columns, 2 * rows):
            score = product(key, q_all[c : c + 2 * rows], 1, 1) * factor + bias
            held[:, c : c + 2 * rows] = score
            top[:, c : c + 2 * rows] = jnp.maximum(
                top[:, c : c + 2 * rows], jnp.max(score, axis=0, keepdims=True)
            )

    @pl.when(phase == 1)
    def _():
        out[...] = jnp.zeros_like(out)
        stats[...] = jnp.zeros_like(stats)
        stats[0:1] = top[...]

    @pl.when(phase == 1)
    def _():
        value = kv[:, DH:]
        for c in range(0, columns, 2 * rows):
            weight = jnp.exp2(held[:, c : c + 2 * rows] - top[:, c : c + 2 * rows])
            stats[1:2, c : c + 2 * rows] += jnp.sum(weight, axis=0, keepdims=True)
            weight = weight.astype(bf16)
            weights[:, c : c + 2 * rows] = weight
            out[:, c : c + 2 * rows] += product(value, weight, 0, 0)


def merge_kernel(grad0, grad1, grad2, grad3, out, stats, grads, packed):
    rows, heads = grad0.shape[1], grad0.shape[0] // DH
    wide = packed.shape[1] // 3
    for g, grad in enumerate([grad0, grad1, grad2, grad3]):
        for h in range(heads):
            at = (g * heads + h) * rows
            to = slice(at, at + rows)
            part = grad[h * DH : (h + 1) * DH]
            grads[:, to] = part
            row, column = at // wide, at % wide
            for k, value in enumerate(
                [stats[0:1, to], stats[1:2, to], jnp.sum(part.astype(f32) * out[:, to], axis=0, keepdims=True)]
            ):
                packed[row : row + 1, k * wide + column : k * wide + column + rows] = value


def backward_kernel(
    q0, q1, q2, q3, grads_in, stats0, stats1, stats2, stats3, kv, weights,
    kv_part, own, part1, part2, part3,
    q_all, grads, delta, score_grad, kv_near, sems,
):
    rows, heads = q0.shape[0], q0.shape[1] // DH
    columns = q_all.shape[0]
    wide = heads * rows
    scale = 1.0 / math.sqrt(DH)
    stack_heads(q_all, [q0, q1, q2, q3])
    every = [stats0, stats1, stats2, stats3]
    lanes = stats0.shape[1] // 3
    each = wide // lanes
    for g in range(len(every)):
        views = [stats[(g ^ m) * each : (g ^ m) * each + each] for m, stats in enumerate(every)]
        tops = [view[:, :lanes] for view in views]
        peak = functools.reduce(jnp.maximum, tops)
        gains = [jnp.exp2(top - peak) for top in tops]
        mass = sum(view[:, lanes : 2 * lanes] * up for view, up in zip(views, gains))
        dots = sum(view[:, 2 * lanes :] * up for view, up in zip(views, gains))
        inverse = 1.0 / mass
        near = gains[0] * inverse
        middle = near * dots * inverse
        for r in range(each):
            to = slice(g * wide + r * lanes, g * wide + (r + 1) * lanes)
            delta[:, to] = middle[r : r + 1]
            grads[:, to] = (grads_in[:, to].astype(f32) * near[r : r + 1]).astype(bf16)

    key, value = kv[:, :DH], kv[:, DH:]
    leaves = []
    for r in range(0, key.shape[0], 2 * rows):
        block = slice(r, r + 2 * rows)
        for c in range(0, columns, 2 * rows):
            at = slice(c, c + 2 * rows)
            prob_grad = product(value[block], grads[:, at])
            weight = weights[block, at].astype(f32)
            score_grad[block, at] = (weight * (prob_grad - delta[:, at])).astype(bf16)
        kv_near[block, DH:] = product(weights[block], grads[...], 1, 1).astype(bf16)
        kv_near[block, :DH] = (product(score_grad[block], q_all[...]) * scale).astype(bf16)
        part_rows = pl.ds(r, 2 * rows)
        leaves.append(
            pltpu.make_async_copy(
                kv_near.at[part_rows], kv_part.at[part_rows], sems.at[r // (2 * rows)]
            )
        )
        leaves[-1].start()
    for g, part in enumerate([own, part1, part2, part3]):
        total = product(key, score_grad[:, g * wide : (g + 1) * wide], 0, 0)
        for h in range(heads):
            moved = total[:, h * rows : (h + 1) * rows].T * scale
            part[:, h * DH : (h + 1) * DH] = moved.astype(part.dtype)
    for leave in leaves:
        leave.wait()


def final_kernel(flags, own, lower, upper, both, key_grad, value_grad):
    same = own[...].astype(f32) + upper[...].astype(f32)
    rest = lower[...].astype(f32) + both[...].astype(f32)
    low = flags[1:2, 0:1] == 0.0
    first, second = jnp.where(low, same, rest), jnp.where(low, rest, same)
    for k, summed in enumerate([first, second]):
        key_grad[:, k * DH : (k + 1) * DH] = summed[:, :DH].astype(bf16)
        value_grad[:, k * DH : (k + 1) * DH] = summed[:, DH:].astype(bf16)


def across(array, axis, mask=1):
    count = lax.axis_size(axis)
    return lax.ppermute(array, axis, [(i, i ^ mask) for i in range(count)])


def shared(array):
    return [array] + [across(array, CLIQUE, mask) for mask in (1, 2, 3)]


def on_device(
    resid, out_grad, norm_gain, expert_ids, combine, w_gate, w_up, w_down, w_out,
    queries, keys, values, span_order,
):
    rows, width = resid.shape
    heads = queries.shape[1] // DH
    hidden = w_gate.shape[1]
    n_y, n_x, n_hi, n_lh, n_lb = (lax.axis_size(axis) for axis in ("y", "x", "hi", "lh", "lb"))
    core, high, share = lax.axis_index("core"), lax.axis_index("hi"), lax.axis_index(CLIQUE)
    n_share = 2 * n_lb
    chunk = rows // (n_lh * n_share)
    half = width // 2
    columns = n_share * heads * rows
    n_keys = n_y * n_x * n_hi * n_lh * chunk
    place = jnp.stack([lax.axis_index(CTX), share]).astype(jnp.int32)
    group = lax.axis_index("lh")
    bits = jnp.stack([core, group, lax.axis_index("lb")])
    flags = jnp.broadcast_to(bits[:, None], (3, 128)).astype(f32)

    give, keep, selector, resid16, grad16, gain, own_kv, leaving = pl.pallas_call(
        expert_kernel,
        out_shape=(
            shape((CAP, half), bf16),
            shape((CAP, half), f32),
            shape((CAP, rows), bf16),
            shape((CAP, width), bf16),
            shape((CAP, width), bf16),
            shape((1, width), f32),
            shape((n_lh, chunk, 2 * DH), bf16),
            shape((n_lh, chunk, 2 * DH), bf16),
        ),
        in_specs=[VMEM] + [HBM] * 10,
        out_specs=(VMEM,) * 8,
        scratch_shapes=[
            pltpu.VMEM(expert_ids.shape[::-1], jnp.int32),
            pltpu.VMEM(expert_ids.shape[::-1], f32),
            pltpu.VMEM((rows, width), bf16),
            pltpu.VMEM((rows, width), bf16),
            pltpu.VMEM((2 * hidden, width), bf16),
            pltpu.VMEM((hidden, width), bf16),
            pltpu.VMEM(keys.shape, bf16),
            pltpu.VMEM(values.shape, bf16),
            pltpu.SemaphoreType.DMA((19,)),
        ],
        compiler_params=params(24),
        cost_estimate=cost(10 * CAP * width * hidden, 8 << 20),
        name="expert",
    )(
        flags,
        *map(
            stay,
            (expert_ids.T, combine.T, norm_gain[None, :], resid, out_grad)
            + (w_gate.T, w_up.T, w_down, keys, values),
        ),
    )

    far_kv = across(leaving, ("hi", "lh"), 3)
    plane_kv = jnp.where(high == 0, jnp.stack([own_kv, far_kv]), jnp.stack([far_kv, own_kv]))
    sent = jnp.broadcast_to(plane_kv[None], (n_y * n_x,) + plane_kv.shape)

    pair = lax.optimization_barrier((keep + across(give, "core").astype(f32)).astype(bf16))
    kv = lax.all_to_all(sent, PLANE, 0, 0, tiled=True).reshape(-1, 2 * DH)
    r1, r2, r3 = [across(pair, ("lh", "lb"), mask) for mask in (1, 2, 3)]
    total = (pair.astype(f32) + r1.astype(f32)) + (r2.astype(f32) + r3.astype(f32))
    total = lax.optimization_barrier(total.astype(bf16))
    other = across(total, "core")
    resid_grad, attn_grad = pl.pallas_call(
        late_kernel,
        out_shape=(shape((rows, width), bf16), shape((heads * DH, rows), bf16)),
        in_specs=[VMEM] * 7 + [HBM] * 2,
        out_specs=(HBM, VMEM),
        scratch_shapes=[
            pltpu.VMEM((rows, width), bf16),
            pltpu.VMEM((rows, width), bf16),
            pltpu.VMEM(w_out.shape, bf16),
            pltpu.SemaphoreType.DMA((4,)),
        ],
        compiler_params=params(16),
        cost_estimate=cost(1 << 20, 1 << 16),
        name="late",
    )(flags, total, other, resid16, grad16, gain, selector, stay(out_grad), stay(w_out))

    query_all = shared(queries)
    tour = itertools.product(range(n_y), range(n_x))
    held = [
        ((y * n_hi + hi) * n_x + x, i) for y, x in tour for hi in range(n_hi) for i in range(n_lh)
    ]
    whole = lambda *_: (0, 0)
    pair_flops = 2 * n_keys * columns * DH
    weights, out, stats = pl.pallas_call(
        functools.partial(forward_kernel, chunk, held),
        grid=(2,),
        out_shape=(
            shape((n_keys, columns), bf16),
            shape((DH, columns), f32),
            shape((8, columns), f32),
        ),
        in_specs=[SMEM, SMEM] + [pl.BlockSpec((rows, heads * DH), whole)] * n_share
        + [pl.BlockSpec((n_keys, 2 * DH), whole)],
        out_specs=(
            pl.BlockSpec((n_keys, columns), whole),
            pl.BlockSpec((DH, columns), whole),
            pl.BlockSpec((8, columns), whole),
        ),
        scratch_shapes=[
            pltpu.VMEM((columns, DH), bf16),
            pltpu.VMEM((n_keys, columns), f32),
            pltpu.VMEM((1, columns), f32),
        ],
        compiler_params=params(24),
        cost_estimate=cost(2 * pair_flops, 6 << 20),
        name="forward",
    )(place, span_order, *query_all, kv)
    grads, packed = pl.pallas_call(
        merge_kernel,
        out_shape=(shape((DH, columns), bf16), shape((8, 3 * columns // 8), f32)),
        in_specs=[VMEM] * (n_share + 2),
        out_specs=(VMEM, VMEM),
        compiler_params=params(12),
        cost_estimate=cost(2 * DH * columns, 3 << 20),
        name="merge",
    )(*shared(attn_grad), out, stats)
    kv_part, query_own, *query_give = pl.pallas_call(
        backward_kernel,
        out_shape=(shape((n_keys, 2 * DH), bf16), shape((rows, heads * DH), f32))
        + (shape((rows, heads * DH), bf16),) * (n_share - 1),
        in_specs=[VMEM] * (2 * n_share + 3),
        out_specs=(HBM,) + (VMEM,) * n_share,
        scratch_shapes=[
            pltpu.VMEM((columns, DH), bf16),
            pltpu.VMEM((DH, columns), bf16),
            pltpu.VMEM((1, columns), f32),
            pltpu.VMEM((n_keys, columns), bf16),
            pltpu.VMEM((n_keys, 2 * DH), bf16),
            pltpu.SemaphoreType.DMA((n_keys // (2 * rows),)),
        ],
        compiler_params=params(16),
        cost_estimate=cost(4 * pair_flops, 8 << 20),
        name="backward",
    )(*query_all, grads, *shared(packed), kv, weights)
    got = lax.all_to_all(
        kv_part.reshape(n_y * n_x, n_hi * n_lh * chunk, 2 * DH), PLANE, 0, 0, tiled=True
    )
    query_parts = [
        across(part, CLIQUE, mask).astype(f32) for mask, part in enumerate(query_give, 1)
    ]
    query_grad = (query_own + sum(query_parts)).astype(bf16)

    owned = jnp.sum(got.astype(f32), axis=0).astype(bf16)
    owned = owned.reshape(n_hi * n_lh, chunk, 2 * DH)
    here = 2 * high + group
    parts = [lax.dynamic_index_in_dim(owned, here, 0, keepdims=False)] + [
        across(lax.dynamic_index_in_dim(owned, here ^ mask, 0, keepdims=False), ("hi", "lh"), mask)
        for mask in (1, 2, 3)
    ]
    key_grad, value_grad = pl.pallas_call(
        final_kernel,
        out_shape=(shape((chunk, n_lh * DH), bf16),) * 2,
        in_specs=[VMEM] * 5,
        out_specs=(VMEM, VMEM),
        compiler_params=params(8),
        name="final",
    )(flags, *parts)
    return (resid_grad, query_grad, key_grad, value_grad)


def solution(mesh):
    fine = Mesh(mesh.devices.reshape(4, 2, 4, 2, 2, 2), CTX + EXP)
    return jax.shard_map(
        on_device,
        mesh=fine,
        in_specs=(
            P(CTX, None),
            P(CTX, None),
            P(),
            P(CTX, None),
            P(CTX, None),
            P(None, EXP),
            P(None, EXP),
            P(EXP, None),
            P(EXP, None),
            P(CTX, EXP),
            P(CTX, None),
            P(CTX, None),
            P(),
        ),
        out_specs=(
            P(CTX, None),
            P(CTX, EXP),
            P(CTX + EXP, None),
            P(CTX + EXP, None),
        ),
        check_vma=False,
    )
```

```python
import functools
import itertools
import math

import jax
import jax.numpy as jnp
from jax import lax
from jax.experimental import pallas as pl
from jax.experimental.pallas import tpu as pltpu
from jax.sharding import Mesh, PartitionSpec as P

DH = 128
GROUP = 16
CAP = 16
EPS = 1e-06
LOW = -1e30
AHEAD = 8
CTX = ("y", "hi", "x")
EXP = ("lh", "lb", "core")
CLIQUE = ("lb", "core")
PLANE = ("y", "x")

bf16 = jnp.bfloat16
f32 = jnp.float32
SMEM = pl.BlockSpec(memory_space=pltpu.SMEM)
VMEM = pl.BlockSpec(memory_space=pltpu.VMEM)
HBM = pl.BlockSpec(memory_space=pltpu.HBM)


def product(left, right, left_dim=1, right_dim=0):
    return lax.dot_general(
        left, right, (((left_dim,), (right_dim,)), ((), ())), preferred_element_type=f32
    )


def params(mib):
    return pltpu.CompilerParams(vmem_limit_bytes=mib << 20)


def cost(flops, moved):
    return pl.CostEstimate(flops=flops, bytes_accessed=moved, transcendentals=0)


def stay(array):
    return pltpu.with_memory_space_constraint(array, pltpu.HBM)


def shape(dims, dtype):
    return jax.ShapeDtypeStruct(dims, dtype)


def expert_kernel(
    flags, ids_far, combine_far, gain_far, resid, out_grad, w_gate, w_up, w_down,
    keys, values, give, keep, selector, resid16, grad16, gain, own_kv, leaving_kv,
    ids, combine, resid_in, grad_in, wide_in, down_in, keys_in, values_in, sems,
):
    hidden_rows = w_down.shape[0]
    cuts = (sems.shape[0] - 7) // 3
    step = w_down.shape[1] // cuts
    heads = [
        pltpu.make_async_copy(source, target, sems.at[i])
        for i, (source, target) in enumerate(
            [
                (ids_far, ids),
                (combine_far, combine),
                (gain_far, gain),
                (resid, resid_in),
                (out_grad, grad_in),
                (keys, keys_in),
                (values, values_in),
            ]
        )
    ]
    spans = [pl.ds(i * step, step) for i in range(cuts)]
    bodies = [
        [
            pltpu.make_async_copy(
                source.at[:, span], target.at[pl.ds(row, hidden_rows), span], sems.at[7 + 3 * i + j]
            )
            for j, (source, target, row) in enumerate(
                [(w_gate, wide_in, 0), (w_up, wide_in, hidden_rows), (w_down, down_in, 0)]
            )
        ]
        for i, span in enumerate(spans)
    ]
    for copy in heads:
        copy.start()
    for body in bodies[:AHEAD]:
        for copy in body:
            copy.start()
    for copy in heads[:3] + heads[5:]:
        copy.wait()
    core, high_head, upper_pair = [flags[i : i + 1, 0:1] > 0.5 for i in range(3)]
    chunk = own_kv.shape[1]
    for i in range(own_kv.shape[0]):
        for side, source in enumerate((keys_in, values_in)):
            p = [source[(4 * i + k) * chunk : (4 * i + k + 1) * chunk] for k in range(4)]
            mine = jnp.where(upper_pair, jnp.where(core, p[3], p[2]), jnp.where(core, p[1], p[0]))
            left, right = mine[:, :DH], mine[:, DH:]
            to = slice(side * DH, (side + 1) * DH)
            own_kv[i, :, to] = jnp.where(high_head, right, left)
            leaving_kv[i, :, to] = jnp.where(high_head, left, right)
    rows = ids.shape[1]
    hit = ids[...] == 0
    chosen_row = jnp.sum(jnp.where(hit, 1.0, 0.0), axis=0, keepdims=True)
    weight_row = jnp.sum(jnp.where(hit, combine[...], 0.0), axis=0, keepdims=True)
    before = lax.broadcasted_iota(jnp.int32, (rows, rows), 0)
    after = lax.broadcasted_iota(jnp.int32, (rows, rows), 1)
    upper = jnp.where(before <= after, 1.0, 0.0).astype(bf16)
    spread = jnp.broadcast_to(chosen_row, (CAP, rows)).astype(bf16)
    rank_row = product(spread, upper)
    slot = lax.broadcasted_iota(jnp.int32, (CAP, rows), 0).astype(f32) + 1.0
    picks = (rank_row == slot) & (chosen_row > 0.0)
    pick = jnp.where(picks, 1.0, 0.0).astype(bf16)
    selector[...] = pick
    weight16 = jnp.sum(jnp.where(picks, weight_row, 0.0), axis=1, keepdims=True)
    heads[3].wait()
    rows16 = product(pick, resid_in[...])
    resid16[...] = rows16.astype(bf16)
    rms16 = lax.rsqrt(jnp.mean(rows16 * rows16, axis=1, keepdims=True) + EPS)
    normed16 = (rows16 * rms16 * gain[...]).astype(bf16)
    heads[4].wait()
    taken = product(pick, grad_in[...])
    grad16[...] = taken.astype(bf16)
    scaled16 = (taken * weight16).astype(bf16)
    pre = hidden = 0.0
    for i, span in enumerate(spans):
        for copy in bodies[i]:
            copy.wait()
        if i + AHEAD < cuts:
            for copy in bodies[i + AHEAD]:
                copy.start()
        at = slice(i * step, (i + 1) * step)
        pre += product(normed16[:, at], wide_in[:, span], 1, 1)
        hidden += product(scaled16[:, at], down_in[:, span], 1, 1)
    pre, hidden = pre.T, hidden.T
    gate_pre, up_pre = pre[:hidden_rows], pre[hidden_rows:]
    sig = jax.nn.sigmoid(gate_pre)
    gate_grad = hidden * up_pre * sig * (1.0 + gate_pre * (1.0 - sig))
    up_grad = hidden * gate_pre * sig
    both = jnp.concatenate([gate_grad, up_grad], axis=0).astype(bf16)
    half = give.shape[1]
    first = product(both, wide_in[:, :half], 0, 0)
    second = product(both, wide_in[:, half:], 0, 0)
    low = flags[0:1, 0:1] == 0.0
    keep[...] = jnp.where(low, first, second)
    give[...] = jnp.where(low, second, first).astype(bf16)


def late_kernel(
    flags, summed, other, resid16, grad16, gain, selector, out_grad, w_out,
    resid_grad, attn_grad, merged, grad_in, out_in, sems,
):
    cuts = sems.shape[0] - 2
    step = w_out.shape[1] // cuts
    arrive = pltpu.make_async_copy(out_grad, grad_in, sems.at[cuts])
    arrive.start()
    spans = [pl.ds(i * step, step) for i in range(cuts)]
    copies = [
        pltpu.make_async_copy(w_out.at[:, span], out_in.at[:, span], sems.at[i])
        for i, span in enumerate(spans)
    ]
    for copy in copies[:AHEAD]:
        copy.start()
    low = flags[0:1, 0:1] == 0.0
    first, second = summed[...].astype(f32), other[...].astype(f32)
    left, right = jnp.where(low, first, second), jnp.where(low, second, first)
    gained = jnp.concatenate([left, right], axis=1) * gain[...]
    wide = resid16[...].astype(f32)
    rms = lax.rsqrt(jnp.mean(wide * wide, axis=1, keepdims=True) + EPS)
    inner = jnp.mean(gained * wide, axis=1, keepdims=True)
    done = (grad16[...].astype(f32) + rms * (gained - wide * rms * rms * inner)).astype(bf16)
    pick = selector[...]
    chosen = product(pick, jnp.ones((CAP, 128), bf16), 0, 0)[:, :1] > 0.5
    moved = product(pick, done, 0, 0).astype(bf16)
    arrive.wait()
    merged[...] = jnp.where(chosen, moved, grad_in[...])
    leave = pltpu.make_async_copy(merged, resid_grad, sems.at[cuts + 1])
    leave.start()
    total = 0.0
    for i, span in enumerate(spans):
        copies[i].wait()
        if i + AHEAD < cuts:
            copies[i + AHEAD].start()
        total += product(out_in[:, span], merged[:, span], 1, 1)
    attn_grad[...] = total.astype(bf16)
    leave.wait()


def stack_heads(target, groups):
    rows, heads = groups[0].shape[0], groups[0].shape[1] // DH
    for g, group in enumerate(groups):
        for h in range(heads):
            at = (g * heads + h) * rows
            target[at : at + rows] = group[:, h * DH : (h + 1) * DH]


def forward_kernel(
    chunk, order, place, spans, q0, q1, q2, q3, kv, weights, out, stats, q_all, held, top
):
    phase = pl.program_id(0)
    rows = q0.shape[0]
    block = rows // 2
    columns = q_all.shape[0]
    factor = math.log2(math.e) / math.sqrt(DH)

    @pl.when(phase == 0)
    def _():
        stack_heads(q_all, [q0, q1, q2, q3])
        top[...] = jnp.full_like(top, 2.0 * LOW)

    @pl.when(phase == 0)
    def _():
        lane = lax.broadcasted_iota(jnp.int32, (chunk, rows), 1)
        below = lax.broadcasted_iota(jnp.int32, (chunk, rows), 0)
        here = place[0] * 2
        query_pos = jnp.where(
            lane < block, spans[here] * block + lane, spans[here + 1] * block + lane - block
        )
        pieces = []
        for ctx, i in order:
            key_pos = spans[2 * ctx + i] * block + place[1] * chunk + below
            pieces.append(jnp.where(key_pos <= query_pos, 0.0, LOW))
        bias = jnp.concatenate(pieces, axis=0)
        bias = jnp.concatenate([bias, bias], axis=1)
        key = kv[:, :DH]
        for c in range(0, columns, 2 * rows):
            score = product(key, q_all[c : c + 2 * rows], 1, 1) * factor + bias
            held[:, c : c + 2 * rows] = score
            top[:, c : c + 2 * rows] = jnp.maximum(
                top[:, c : c + 2 * rows], jnp.max(score, axis=0, keepdims=True)
            )

    @pl.when(phase == 1)
    def _():
        out[...] = jnp.zeros_like(out)
        stats[...] = jnp.zeros_like(stats)
        stats[0:1] = top[...]

    @pl.when(phase == 1)
    def _():
        value = kv[:, DH:]
        for c in range(0, columns, 2 * rows):
            weight = jnp.exp2(held[:, c : c + 2 * rows] - top[:, c : c + 2 * rows])
            stats[1:2, c : c + 2 * rows] += jnp.sum(weight, axis=0, keepdims=True)
            weight = weight.astype(bf16)
            weights[:, c : c + 2 * rows] = weight
            out[:, c : c + 2 * rows] += product(value, weight, 0, 0)


def merge_kernel(grad0, grad1, grad2, grad3, out, stats, grads, packed):
    rows, heads = grad0.shape[1], grad0.shape[0] // DH
    wide = packed.shape[1] // 3
    for g, grad in enumerate([grad0, grad1, grad2, grad3]):
        for h in range(heads):
            at = (g * heads + h) * rows
            to = slice(at, at + rows)
            part = grad[h * DH : (h + 1) * DH]
            grads[:, to] = part
            row, column = at // wide, at % wide
            for k, value in enumerate(
                [stats[0:1, to], stats[1:2, to], jnp.sum(part.astype(f32) * out[:, to], axis=0, keepdims=True)]
            ):
                packed[row : row + 1, k * wide + column : k * wide + column + rows] = value


def backward_kernel(
    q0, q1, q2, q3, grads_in, stats0, stats1, stats2, stats3, kv, weights,
    kv_part, own, part1, part2, part3,
    q_all, grads, delta, score_grad, kv_near, sems,
):
    rows, heads = q0.shape[0], q0.shape[1] // DH
    columns = q_all.shape[0]
    wide = heads * rows
    scale = 1.0 / math.sqrt(DH)
    stack_heads(q_all, [q0, q1, q2, q3])
    every = [stats0, stats1, stats2, stats3]
    lanes = stats0.shape[1] // 3
    each = wide // lanes
    for g in range(len(every)):
        views = [stats[(g ^ m) * each : (g ^ m) * each + each] for m, stats in enumerate(every)]
        tops = [view[:, :lanes] for view in views]
        peak = functools.reduce(jnp.maximum, tops)
        gains = [jnp.exp2(top - peak) for top in tops]
        mass = sum(view[:, lanes : 2 * lanes] * up for view, up in zip(views, gains))
        dots = sum(view[:, 2 * lanes :] * up for view, up in zip(views, gains))
        inverse = 1.0 / mass
        near = gains[0] * inverse
        middle = near * dots * inverse
        for r in range(each):
            to = slice(g * wide + r * lanes, g * wide + (r + 1) * lanes)
            delta[:, to] = middle[r : r + 1]
            grads[:, to] = (grads_in[:, to].astype(f32) * near[r : r + 1]).astype(bf16)

    key, value = kv[:, :DH], kv[:, DH:]
    leaves = []
    for r in range(0, key.shape[0], 2 * rows):
        block = slice(r, r + 2 * rows)
        for c in range(0, columns, 2 * rows):
            at = slice(c, c + 2 * rows)
            prob_grad = product(value[block], grads[:, at])
            weight = weights[block, at].astype(f32)
            score_grad[block, at] = (weight * (prob_grad - delta[:, at])).astype(bf16)
        kv_near[block, DH:] = product(weights[block], grads[...], 1, 1).astype(bf16)
        kv_near[block, :DH] = (product(score_grad[block], q_all[...]) * scale).astype(bf16)
        part_rows = pl.ds(r, 2 * rows)
        leaves.append(
            pltpu.make_async_copy(
                kv_near.at[part_rows], kv_part.at[part_rows], sems.at[r // (2 * rows)]
            )
        )
        leaves[-1].start()
    for g, part in enumerate([own, part1, part2, part3]):
        total = product(key, score_grad[:, g * wide : (g + 1) * wide], 0, 0)
        for h in range(heads):
            moved = total[:, h * rows : (h + 1) * rows].T * scale
            part[:, h * DH : (h + 1) * DH] = moved.astype(part.dtype)
    for leave in leaves:
        leave.wait()


def final_kernel(flags, own, lower, upper, both, key_grad, value_grad):
    same = own[...].astype(f32) + upper[...].astype(f32)
    rest = lower[...].astype(f32) + both[...].astype(f32)
    low = flags[1:2, 0:1] == 0.0
    first, second = jnp.where(low, same, rest), jnp.where(low, rest, same)
    for k, summed in enumerate([first, second]):
        key_grad[:, k * DH : (k + 1) * DH] = summed[:, :DH].astype(bf16)
        value_grad[:, k * DH : (k + 1) * DH] = summed[:, DH:].astype(bf16)


def across(array, axis, mask=1):
    count = lax.axis_size(axis)
    return lax.ppermute(array, axis, [(i, i ^ mask) for i in range(count)])


def shared(array):
    return [array] + [across(array, CLIQUE, mask) for mask in (1, 2, 3)]


def on_device(
    resid, out_grad, norm_gain, expert_ids, combine, w_gate, w_up, w_down, w_out,
    queries, keys, values, span_order,
):
    rows, width = resid.shape
    heads = queries.shape[1] // DH
    hidden = w_gate.shape[1]
    n_y, n_x, n_hi, n_lh, n_lb = (lax.axis_size(axis) for axis in ("y", "x", "hi", "lh", "lb"))
    core, high, share = lax.axis_index("core"), lax.axis_index("hi"), lax.axis_index(CLIQUE)
    n_share = 2 * n_lb
    chunk = rows // (n_lh * n_share)
    half = width // 2
    columns = n_share * heads * rows
    n_keys = n_y * n_x * n_hi * n_lh * chunk
    place = jnp.stack([lax.axis_index(CTX), share]).astype(jnp.int32)
    group = lax.axis_index("lh")
    bits = jnp.stack([core, group, lax.axis_index("lb")])
    flags = jnp.broadcast_to(bits[:, None], (3, 128)).astype(f32)

    give, keep, selector, resid16, grad16, gain, own_kv, leaving = pl.pallas_call(
        expert_kernel,
        out_shape=(
            shape((CAP, half), bf16),
            shape((CAP, half), f32),
            shape((CAP, rows), bf16),
            shape((CAP, width), bf16),
            shape((CAP, width), bf16),
            shape((1, width), f32),
            shape((n_lh, chunk, 2 * DH), bf16),
            shape((n_lh, chunk, 2 * DH), bf16),
        ),
        in_specs=[VMEM] + [HBM] * 10,
        out_specs=(VMEM,) * 8,
        scratch_shapes=[
            pltpu.VMEM(expert_ids.shape[::-1], jnp.int32),
            pltpu.VMEM(expert_ids.shape[::-1], f32),
            pltpu.VMEM((rows, width), bf16),
            pltpu.VMEM((rows, width), bf16),
            pltpu.VMEM((2 * hidden, width), bf16),
            pltpu.VMEM((hidden, width), bf16),
            pltpu.VMEM(keys.shape, bf16),
            pltpu.VMEM(values.shape, bf16),
            pltpu.SemaphoreType.DMA((31,)),
        ],
        compiler_params=params(24),
        cost_estimate=cost(10 * CAP * width * hidden, 8 << 20),
        name="expert",
    )(
        flags,
        *map(
            stay,
            (expert_ids.T, combine.T, norm_gain[None, :], resid, out_grad)
            + (w_gate.T, w_up.T, w_down, keys, values),
        ),
    )

    far_kv = across(leaving, ("hi", "lh"), 3)
    plane_kv = jnp.where(high == 0, jnp.stack([own_kv, far_kv]), jnp.stack([far_kv, own_kv]))
    sent = jnp.broadcast_to(plane_kv[None], (n_y * n_x,) + plane_kv.shape)

    pair = lax.optimization_barrier((keep + across(give, "core").astype(f32)).astype(bf16))
    kv = lax.all_to_all(sent, PLANE, 0, 0, tiled=True).reshape(-1, 2 * DH)
    r1, r2, r3 = [across(pair, ("lh", "lb"), mask) for mask in (1, 2, 3)]
    total = (pair.astype(f32) + r1.astype(f32)) + (r2.astype(f32) + r3.astype(f32))
    total = lax.optimization_barrier(total.astype(bf16))
    other = across(total, "core")
    resid_grad, attn_grad = pl.pallas_call(
        late_kernel,
        out_shape=(shape((rows, width), bf16), shape((heads * DH, rows), bf16)),
        in_specs=[VMEM] * 7 + [HBM] * 2,
        out_specs=(HBM, VMEM),
        scratch_shapes=[
            pltpu.VMEM((rows, width), bf16),
            pltpu.VMEM((rows, width), bf16),
            pltpu.VMEM(w_out.shape, bf16),
            pltpu.SemaphoreType.DMA((4,)),
        ],
        compiler_params=params(16),
        cost_estimate=cost(1 << 20, 1 << 16),
        name="late",
    )(flags, total, other, resid16, grad16, gain, selector, stay(out_grad), stay(w_out))

    query_all = shared(queries)
    tour = itertools.product(range(n_y), range(n_x))
    held = [
        ((y * n_hi + hi) * n_x + x, i) for y, x in tour for hi in range(n_hi) for i in range(n_lh)
    ]
    whole = lambda *_: (0, 0)
    pair_flops = 2 * n_keys * columns * DH
    weights, out, stats = pl.pallas_call(
        functools.partial(forward_kernel, chunk, held),
        grid=(2,),
        out_shape=(
            shape((n_keys, columns), bf16),
            shape((DH, columns), f32),
            shape((8, columns), f32),
        ),
        in_specs=[SMEM, SMEM] + [pl.BlockSpec((rows, heads * DH), whole)] * n_share
        + [pl.BlockSpec((n_keys, 2 * DH), whole)],
        out_specs=(
            pl.BlockSpec((n_keys, columns), whole),
            pl.BlockSpec((DH, columns), whole),
            pl.BlockSpec((8, columns), whole),
        ),
        scratch_shapes=[
            pltpu.VMEM((columns, DH), bf16),
            pltpu.VMEM((n_keys, columns), f32),
            pltpu.VMEM((1, columns), f32),
        ],
        compiler_params=params(24),
        cost_estimate=cost(2 * pair_flops, 6 << 20),
        name="forward",
    )(place, span_order, *query_all, kv)
    grads, packed = pl.pallas_call(
        merge_kernel,
        out_shape=(shape((DH, columns), bf16), shape((8, 3 * columns // 8), f32)),
        in_specs=[VMEM] * (n_share + 2),
        out_specs=(VMEM, VMEM),
        compiler_params=params(12),
        cost_estimate=cost(2 * DH * columns, 3 << 20),
        name="merge",
    )(*shared(attn_grad), out, stats)
    kv_part, query_own, *query_give = pl.pallas_call(
        backward_kernel,
        out_shape=(shape((n_keys, 2 * DH), bf16), shape((rows, heads * DH), f32))
        + (shape((rows, heads * DH), bf16),) * (n_share - 1),
        in_specs=[VMEM] * (2 * n_share + 3),
        out_specs=(HBM,) + (VMEM,) * n_share,
        scratch_shapes=[
            pltpu.VMEM((columns, DH), bf16),
            pltpu.VMEM((DH, columns), bf16),
            pltpu.VMEM((1, columns), f32),
            pltpu.VMEM((n_keys, columns), bf16),
            pltpu.VMEM((n_keys, 2 * DH), bf16),
            pltpu.SemaphoreType.DMA((n_keys // (2 * rows),)),
        ],
        compiler_params=params(16),
        cost_estimate=cost(4 * pair_flops, 8 << 20),
        name="backward",
    )(*query_all, grads, *shared(packed), kv, weights)
    got = lax.all_to_all(
        kv_part.reshape(n_y * n_x, n_hi * n_lh * chunk, 2 * DH), PLANE, 0, 0, tiled=True
    )
    query_parts = [
        across(part, CLIQUE, mask).astype(f32) for mask, part in enumerate(query_give, 1)
    ]
    query_grad = (query_own + sum(query_parts)).astype(bf16)

    owned = jnp.sum(got.astype(f32), axis=0).astype(bf16)
    owned = owned.reshape(n_hi * n_lh, chunk, 2 * DH)
    here = 2 * high + group
    parts = [lax.dynamic_index_in_dim(owned, here, 0, keepdims=False)] + [
        across(lax.dynamic_index_in_dim(owned, here ^ mask, 0, keepdims=False), ("hi", "lh"), mask)
        for mask in (1, 2, 3)
    ]
    key_grad, value_grad = pl.pallas_call(
        final_kernel,
        out_shape=(shape((chunk, n_lh * DH), bf16),) * 2,
        in_specs=[VMEM] * 5,
        out_specs=(VMEM, VMEM),
        compiler_params=params(8),
        name="final",
    )(flags, *parts)
    return (resid_grad, query_grad, key_grad, value_grad)


def solution(mesh):
    fine = Mesh(mesh.devices.reshape(4, 2, 4, 2, 2, 2), CTX + EXP)
    return jax.shard_map(
        on_device,
        mesh=fine,
        in_specs=(
            P(CTX, None),
            P(CTX, None),
            P(),
            P(CTX, None),
            P(CTX, None),
            P(None, EXP),
            P(None, EXP),
            P(EXP, None),
            P(EXP, None),
            P(CTX, EXP),
            P(CTX, None),
            P(CTX, None),
            P(),
        ),
        out_specs=(
            P(CTX, None),
            P(CTX, EXP),
            P(CTX + EXP, None),
            P(CTX + EXP, None),
        ),
        check_vma=False,
    )
```
